128 devices in a mesh: seq: 8 (over z, x_lo), head: 16 (over x_hi, y, core).
Axes of the slice: x: 4 (x_hi: 2, x_lo: 2; x = x_hi * 2 + x_lo), y: 4, z: 4, core: 2. Of those that a mesh axis runs over, the one named last changes fastest.
Arguments:
- query_rows: bfloat16 [2, 4096, 64, 128], P(None, 'seq', 'head'), may hold values from -96 to 96
- key_rows: bfloat16 [2, 4096, 8, 128], P(None, 'seq'), may hold values from -4 to 4
- value_rows: bfloat16 [2, 4096, 8, 128], P(None, 'seq'), may hold values from -6 to 6
- state_in: bfloat16 [2, 4096, 8, 128], P(None, 'seq'), may hold values from -0.44921875 to 0.44921875
- state_out: bfloat16 [2, 4096, 8, 128], P(None, 'seq'), may hold values from -0.44921875 to 0.44921875
- log_decay: float32 [2, 64, 4096], P(None, 'head', 'seq'), may hold values from -0.75 to 0
- doc_ids: int32 [2, 4096], P(None, 'seq'), may hold values from 0 to 3, never falling along the last dimension, each value on 1 to 2048 neighbouring positions
- norm_gain: float32 [8192], replicated, may hold values from 0.1 to 1.9
Outputs:
- hidden_gap: bfloat16 [2, 4096, 8192], P(None, ('seq', 'head'))
- align_err: float32 [2, 64, 4096], P(None, 'head', 'seq')
The draws below stay inside these ranges and needn't reach their ends.
Inputs may be any that keep to these rules, and one draw needn't show every extreme that they name: `doc_ids`: within each sequence the ids never fall, each document spans 1 to 2048 positions and one spans exactly 2048.
All inputs are finite; a program needn't handle non-finite values.
Results may differ from the reference program's by a relative error of at most 0.0065.
Values may be sent and summed in bfloat16 or wider, within the bound.
A program may use at most 64 MiB of HBM per device.

```python
import math
import jax
import jax.numpy as jnp
import numpy as np
from jax import lax

HEAD_COUNT = 64
KVH = 8
HD = 128
NS = 128
SEQUENCE_LENGTH = 4096
SEQUENCE_COUNT = 2


def base_keys(key):
    raw = jax.random.normal(jax.random.fold_in(key, 100), (SEQUENCE_COUNT, SEQUENCE_LENGTH, KVH, HD), jnp.float32)
    return jnp.clip(raw, -4.0, 4.0)


def draw_key_rows(key, part):
    base = base_keys(key)
    return base.astype(jnp.bfloat16)


def draw_query_rows(key, part):
    key = jax.random.fold_in(key, 2)
    first = jax.random.fold_in(key, 0)
    rows = jnp.clip(jax.random.normal(first, (SEQUENCE_COUNT, SEQUENCE_LENGTH, HEAD_COUNT, HD), jnp.float32), -4.0, 4.0)
    return rows.astype(jnp.bfloat16)


def draw_log_decay(key, part):
    key = jax.random.fold_in(key, 3)
    chosen_index, quick_decay_key, gradual_decay_key, noisy_random_key, spike_random_key, layer_depth_key = jax.random.split(key, 6)
    share = 0.5
    fast = jax.random.uniform(chosen_index, (SEQUENCE_COUNT, HEAD_COUNT, 1), jnp.float32) < share
    fast_rate = jnp.exp(jax.random.uniform(quick_decay_key, (SEQUENCE_COUNT, HEAD_COUNT, 1), jnp.float32, jnp.log(1.0 / 50.0), jnp.log(1.0 / 30.0)))
    slow_rate = jnp.exp(jax.random.uniform(gradual_decay_key, (SEQUENCE_COUNT, HEAD_COUNT, 1), jnp.float32, jnp.log(0.2 / SEQUENCE_LENGTH), jnp.log(1.0 / SEQUENCE_LENGTH)))
    decay_speed = jnp.where(fast, fast_rate, slow_rate)
    noisy_value = jax.random.uniform(noisy_random_key, (SEQUENCE_COUNT, HEAD_COUNT, SEQUENCE_LENGTH), jnp.float32, 0.5, 1.5)
    spike_value = jax.random.uniform(spike_random_key, (SEQUENCE_COUNT, HEAD_COUNT, SEQUENCE_LENGTH), jnp.float32) < 3.0 / SEQUENCE_LENGTH
    layer_depth = jax.random.uniform(layer_depth_key, (SEQUENCE_COUNT, HEAD_COUNT, SEQUENCE_LENGTH), jnp.float32, 0.22, 0.69)
    return -(decay_speed * noisy_value) - jnp.where(spike_value, layer_depth, 0.0)


def steps_of(rng, shape, cuts, least, high):
    level, own = 1.0, jax.random.fold_in(rng, 6)
    for axis_at, parts in cuts:
        draws = jnp.exp(jax.random.uniform(jax.random.fold_in(own, axis_at), (parts,), jnp.float32, least / len(cuts), high / len(cuts)))
        level = level * jnp.repeat(draws, shape[axis_at] // parts).reshape([-1 if axis == axis_at else 1 for axis in range(len(shape))])
    return level


def split_up(amount, total, most, lean):
    portions = [(1 << 20) // math.isqrt(standing ** lean) + 1 for standing in range(2, amount + 1)]
    surplus, given = total - most - (amount - 1), [1] * (amount - 1)
    while surplus > 0:
        candidates = [i for i in range(amount - 1) if given[i] < most]
        pool, budget = sum([portions[i] for i in candidates]), surplus
        for i in candidates:
            more = min(most - given[i], max(1, budget * portions[i] // pool), surplus)
            given[i] = given[i] + more
            surplus = surplus - more
    return np.array([most] + given)


def ragged_sizes(stream_key, amount, total, limit, slope):
    if amount == 2:
        one = jax.random.randint(stream_key, (), max(1, total - limit), min(limit, total - 1) + 1)
        return jnp.stack([one, total - one])
    sizes = jnp.asarray(split_up(amount, total, limit, slope), jnp.int32)
    couples = (amount - 1) // 2
    source_of, receiver = sizes[1:1 + 2 * couples:2], sizes[2:2 + 2 * couples:2]
    slack = jnp.minimum(source_of - 1, limit - receiver)
    moved = jax.random.randint(jax.random.fold_in(stream_key, 1), (couples,), 0, 1 << 20) % (slack + 1)
    sizes = sizes.at[1:1 + 2 * couples:2].set(source_of - moved).at[2:2 + 2 * couples:2].set(receiver + moved)
    return sizes[jax.random.permutation(jax.random.fold_in(stream_key, 2), amount)]


def normal_values(own_key, extent, width, limit, shards=(), kind=jnp.bfloat16):
    drawn = jax.random.normal(own_key, extent, jnp.float32) * width
    if len(shards) > 0:
        drawn = steps_of(own_key, extent, shards, -0.22, 0.18) * drawn
    return jnp.clip(drawn, min=-limit, max=limit).astype(kind)


def setup_inputs(seed: int = 0) -> dict:
    streams_of = jax.random.split(jax.random.key(seed), 9)
    return {
        "query_rows": draw_query_rows(jax.random.fold_in(streams_of[8], 71), 0),
        "key_rows": draw_key_rows(jax.random.fold_in(streams_of[8], 71), 0),
        "value_rows": normal_values(streams_of[2], (SEQUENCE_COUNT, SEQUENCE_LENGTH, KVH, HD), 1.0, 6.0, ((1, 8),)),
        "state_in": normal_values(streams_of[3], (SEQUENCE_COUNT, SEQUENCE_LENGTH, KVH, NS), 0.075, 0.44921875, ((1, 8),)),
        "state_out": normal_values(streams_of[4], (SEQUENCE_COUNT, SEQUENCE_LENGTH, KVH, NS), 0.075, 0.44921875, ((1, 8),)),
        "log_decay": draw_log_decay(jax.random.fold_in(streams_of[8], 71), 0),
        "doc_ids": jax.vmap(lambda own: jnp.searchsorted(jnp.cumsum(ragged_sizes(own, 4, SEQUENCE_LENGTH, SEQUENCE_LENGTH // 2, 0)), jnp.arange(SEQUENCE_LENGTH), side="right"))(jax.random.split(streams_of[6], SEQUENCE_COUNT)).reshape((SEQUENCE_COUNT, SEQUENCE_LENGTH)).astype(jnp.int32),
        "norm_gain": jnp.clip(1.0 + 0.18 * jax.random.normal(streams_of[7], (HEAD_COUNT * HD,), jnp.float32), 0.1, 1.9),
    }


def reference(query_rows, key_rows, value_rows, state_in, state_out, log_decay, doc_ids, norm_gain):
    group = HEAD_COUNT // KVH
    scale = 1.0 / math.sqrt(HD)
    block = min(512, SEQUENCE_LENGTH)
    blocks = SEQUENCE_LENGTH // block
    cum = jnp.cumsum(log_decay, axis=2)
    positions = jnp.arange(SEQUENCE_LENGTH, dtype=jnp.int32)

    def one_block(index):
        seq_pos = index // (HEAD_COUNT * blocks)
        rest = index % (HEAD_COUNT * blocks)
        head = rest // blocks
        start = rest % blocks * block
        owner = head // group
        query = lax.dynamic_slice(query_rows, (seq_pos, start, head, jnp.int32(0)), (1, block, 1, HD))[0, :, 0]
        keys_all = key_rows[seq_pos, :, owner]
        values_all = value_rows[seq_pos, :, owner]
        inner_all = state_in[seq_pos, :, owner]
        outer = lax.dynamic_slice(state_out, (seq_pos, start, owner, jnp.int32(0)), (1, block, 1, NS))[0, :, 0]
        docs = doc_ids[seq_pos]
        doc_query = lax.dynamic_slice_in_dim(docs, start, block, 0)
        query_pos = start + jnp.arange(block, dtype=jnp.int32)
        visible = (query_pos[:, None] >= positions[None, :]) & (doc_query[:, None] == docs[None, :])
        scores = jnp.dot(query, keys_all.T, preferred_element_type=jnp.float32) * scale
        top = lax.optimization_barrier(jnp.max(jnp.where(visible, scores, -1e+30), axis=1))
        weights = jnp.where(visible, jnp.exp(scores - top[:, None]), 0.0)
        total = lax.optimization_barrier(jnp.sum(weights, axis=1))
        teacher = (jnp.dot(weights.astype(jnp.bfloat16), values_all, preferred_element_type=jnp.float32) / total[:, None]).astype(jnp.bfloat16)
        cum_row = cum[seq_pos, head]
        cum_query = lax.dynamic_slice_in_dim(cum_row, start, block, 0)
        decay = jnp.exp(jnp.where(visible, cum_query[:, None] - cum_row[None, :], -1e+30))
        mixing = decay * jnp.dot(outer, inner_all.T, preferred_element_type=jnp.float32)
        student = jnp.dot(mixing.astype(jnp.bfloat16), values_all, preferred_element_type=jnp.float32).astype(jnp.bfloat16)
        differ = mixing - weights / total[:, None]
        error = lax.optimization_barrier(jnp.sum(differ * differ, axis=1))
        return (teacher, student, error)
    indices = jnp.arange(SEQUENCE_COUNT * HEAD_COUNT * blocks, dtype=jnp.int32)
    teacher, student, error = lax.map(one_block, indices)
    teacher = teacher.reshape(SEQUENCE_COUNT, HEAD_COUNT, SEQUENCE_LENGTH, HD).transpose(0, 2, 1, 3).reshape(SEQUENCE_COUNT, SEQUENCE_LENGTH, HEAD_COUNT * HD)
    student = student.reshape(SEQUENCE_COUNT, HEAD_COUNT, SEQUENCE_LENGTH, HD).transpose(0, 2, 1, 3).reshape(SEQUENCE_COUNT, SEQUENCE_LENGTH, HEAD_COUNT * HD)
    align_err = error.reshape(SEQUENCE_COUNT, HEAD_COUNT, SEQUENCE_LENGTH)
    teach_f = teacher.astype(jnp.float32)
    stud_f = student.astype(jnp.float32)
    teach_ms = lax.optimization_barrier(jnp.mean(teach_f * teach_f, axis=-1, keepdims=True)) + 1e-05
    stud_ms = lax.optimization_barrier(jnp.mean(stud_f * stud_f, axis=-1, keepdims=True)) + 1e-05
    hidden_gap = (norm_gain * stud_f * lax.rsqrt(stud_ms) - teach_f * lax.rsqrt(teach_ms)).astype(jnp.bfloat16)
    return (hidden_gap, align_err)
```

```python
import math

import jax
import jax.numpy as jnp
from jax import lax
from jax.experimental import pallas as pl
from jax.experimental.pallas import tpu as pltpu
from jax.sharding import PartitionSpec as P

F32, BF16 = jnp.float32, jnp.bfloat16
BLK, HG, SLOTS, TQ = 512, 8, 5, 256
UNROLL = 2
XR = 272
LOG2E = 1.4426950408889634
SC = LOG2E / math.sqrt(128.0)
BIG = 1e30
EPS = 1e-05
NT = (((1,), (1,)), ((), ()))
MESH = pl.DeviceIdType.MESH


def dot_nt(a, b):
    return lax.dot_general(a, b, NT, preferred_element_type=F32)


def dot(a, b):
    return jnp.dot(a, b, preferred_element_type=F32)


def fold_sum(x):
    return jnp.sum(x.reshape(x.shape[0] // 8, 8, x.shape[1]), axis=0)


def fold_max(x):
    return jnp.max(jnp.max(x.reshape(x.shape[0] // 8, 8, x.shape[1]), axis=0), axis=0, keepdims=True)


def prefix_sums(x):
    lane = lax.broadcasted_iota(jnp.int32, x.shape, 1)
    step = 1
    while step < x.shape[1]:
        x = x + jnp.where(lane >= step, pltpu.roll(x, step, 1), 0.0)
        step *= 2
    return x


def to_columns(rows):
    wide = jnp.concatenate([rows, jnp.zeros((120, rows.shape[1]), F32)], axis=0)
    return jnp.transpose(wide)


def t16(x):
    return jnp.transpose(x.astype(F32)).astype(BF16)


class Refs:
    pass


class Place:
    def __init__(self):
        self.s, self.hd = lax.axis_index("seq"), lax.axis_index("head")
        self.z, self.col = self.s // 2, self.s % 2
        self.g, self.c = self.hd // 2, self.hd % 2
        self.sibling = (self.s, self.g * 2 + 1 - self.c)
        self.beside = (self.z * 2 + 1 - self.col, self.hd)
        self.above = (self.s + 2, self.hd)
        self.below = (self.s - 2, self.hd)


def remote(src, dst, send, recv, device):
    return pltpu.make_async_remote_copy(
        src_ref=src, dst_ref=dst, send_sem=send, recv_sem=recv, device_id=device, device_id_type=MESH)


def greet(w):
    barrier = pltpu.get_barrier_semaphore()

    def tell(device):
        pl.semaphore_signal(barrier, inc=1, device_id=device, device_id_type=MESH)

    def others(k, _):
        tell((w.s, (w.hd + k) % 16))
        return 0
    lax.fori_loop(1, 16, others, 0)
    tell(w.beside)

    @pl.when(w.z < 3)
    def _():
        tell(w.above)

    @pl.when(w.z > 0)
    def _():
        tell(w.below)
    pl.semaphore_wait(barrier, 16 + (w.z + 2) // 3 + (5 - w.z) // 3 - 0)


def swap_copies(r, w):
    return (remote(r.query.at[1 - w.c], r.qraw.at[1], r.swap_send.at[0], r.swap_recv.at[0], w.sibling),
            remote(r.aux_in.at[1 - w.c], r.aux_raw.at[1], r.swap_send.at[1], r.swap_recv.at[1], w.sibling))


def part(r, slot, j):
    return r.aux.at[slot] if j == 3 else r.kvb.at[slot, j]


def up_copy(r, w, step, j):
    return remote(part(r, 2 * step, j), part(r, 2 * step + 2, j), r.up_send.at[step, j], r.up_recv.at[step, j], w.above)


def side_copy(r, w, step, j):
    return remote(part(r, 2 * step + 2 * w.col, j), part(r, 2 * step + 1, j), r.side_send.at[step, j], r.side_recv.at[step, j], w.beside)


def sends_up(w, step):
    return (w.z < 3) if step == 0 else ((w.z >= 1) & (w.z < 3))


def sends_side(w, step):
    return w.z >= step + w.col


def gets_up(w, step):
    return w.z >= step + 1


def gets_side(w, step):
    return w.z >= step + 1 - w.col


def load_own(r, w):
    loads = [pltpu.make_async_copy(ref.at[w.c], r.raw.at[i], r.load_sem.at[i])
             for i, ref in enumerate((r.key, r.value, r.inner, r.outer))]
    qload = pltpu.make_async_copy(r.query.at[w.c], r.qraw.at[0], r.load_sem.at[4])
    aload = pltpu.make_async_copy(r.aux_in.at[w.c], r.aux_raw.at[0], r.load_sem.at[5])
    aload.start()
    for x in loads:
        x.start()
    qload.start()
    greet(w)
    swaps = swap_copies(r, w)
    swaps[1].start()
    swaps[0].start()

    def send_part(j):
        @pl.when(sends_up(w, 0))
        def _():
            up_copy(r, w, 0, j).start()

        @pl.when((w.col == 0) & sends_side(w, 0))
        def _():
            side_copy(r, w, 0, j).start()

    aload.wait()
    swaps[1].wait_recv()
    mine, theirs = r.aux_raw[0], r.aux_raw[1]
    first = jnp.where(w.c == 0, mine, theirs)
    second = jnp.where(w.c == 0, theirs, mine)
    r.aux[0, 0:8, :] = jnp.concatenate([first[0:4], second[0:4]], axis=0)
    r.aux[0, 8:16, :] = jnp.broadcast_to(mine[4:5], (8, BLK))
    send_part(3)
    for i in range(4):
        loads[i].wait()
        r.wide[...] = r.raw[i].astype(F32)
        rows = r.wide[pl.ds(w.g, BLK, stride=8), :].astype(BF16)
        if i < 3:
            r.kvb[0, i] = rows
            send_part(i)
        else:
            r.outer_own[...] = rows
    qload.wait()
    swaps[0].wait_recv()
    for i in range(2):
        r.wide[0:2048, :] = r.qraw[i].astype(F32)
        base = 4 * w.c if i == 0 else 4 - 4 * w.c
        for j in range(4):
            r.q[base + j] = r.wide[pl.ds(j, BLK, stride=4), :].astype(BF16)
    for x in swaps:
        x.wait_send()


def take_up(r, w, step):
    for j in (3, 0, 1, 2):
        @pl.when(gets_up(w, step))
        def _():
            up_copy(r, w, step, j).wait_recv()
            if step == 0:
                @pl.when(sends_up(w, 1))
                def _():
                    up_copy(r, w, 1, j).start()

                @pl.when(w.col == 0)
                def _():
                    side_copy(r, w, 1, j).start()

                @pl.when(w.col == 1)
                def _():
                    side_copy(r, w, 0, j).start()
            else:
                @pl.when(w.col == 1)
                def _():
                    side_copy(r, w, 1, j).start()


def take_side(r, w, step):
    @pl.when(gets_side(w, step))
    def _():
        for j in range(4):
            side_copy(r, w, step, j).wait_recv()


def end_sends(r, w):
    for step in range(2):
        @pl.when(sends_up(w, step))
        def _():
            for j in range(4):
                up_copy(r, w, step, j).wait_send()

        @pl.when(sends_side(w, step))
        def _():
            for j in range(4):
                side_copy(r, w, step, j).wait_send()


def own_prepare(r):
    own = prefix_sums(r.aux[0, 0:8, :])
    r.csum[...] = own
    r.csum_col[...] = to_columns(own)
    doc_c = to_columns(r.aux[0, 8:16, :])[:, 0:1]
    cb = dot_nt(r.kvb[0, 2], r.outer_own[...])
    kj = lax.broadcasted_iota(jnp.int32, (BLK, BLK), 0)
    qi = lax.broadcasted_iota(jnp.int32, (BLK, BLK), 1)
    seen = (qi >= kj) & (doc_c == r.aux[0, 8:9, :])
    r.cb[...] = jnp.where(seen, cb, 0.0)
    r.hide[...] = jnp.where(seen, 0.0, -BIG)
    r.xt[0:128, :] = t16(r.kvb[0, 1])
    r.xt[256:XR, :] = jnp.ones((XR - 256, BLK), BF16)
    r.vo[0:128, :] = r.xt[0:128, :]
    r.vo[128:144, :] = jnp.ones((16, BLK), BF16)
    r.tail[...] = jnp.zeros((8, 128), F32)


def own_block(r):
    def head(h, _):
        lanes = lax.broadcasted_iota(jnp.int32, (BLK, 128), 1)
        acol = jnp.sum(jnp.where(lanes == h, r.csum_col[...], 0.0), axis=1, keepdims=True)
        arow = r.csum[pl.ds(h, 1), :]
        for qt in range(BLK // TQ):
            cols = slice(qt * TQ, (qt + 1) * TQ)
            n = (qt + 1) * TQ
            s = dot_nt(r.kvb[0, 0, 0:n, :], r.q[h, cols, :]) + r.hide[0:n, cols]
            m = fold_max(s)
            p = jnp.exp2((s - m) * SC)
            mix = jnp.exp2(jnp.minimum((arow[:, cols] - acol[0:n]) * LOG2E, 0.0)) * r.cb[0:n, cols]
            av = dot(r.vo[:, 0:n], p.astype(BF16))
            r.m[h, :, cols] = jnp.broadcast_to(m, (8, TQ))
            r.sq[h, :, cols] = fold_sum(p * p)
            r.cross[h, :, cols] = fold_sum(p * mix)
            r.mixsq[h, :, cols] = fold_sum(mix * mix)
            r.acc[h, 0:128, cols] = av[0:128]
            r.acc[h, 128:256, cols] = jnp.zeros((128, TQ), F32)
            r.acc[h, 256:XR, cols] = av[128:144]
            r.stud[h, :, cols] = dot(r.vo[0:128, 0:n], mix.astype(BF16))
        r.state[h] = jnp.zeros((256, 128), F32)
        return 0
    lax.fori_loop(0, HG, head, 0)


def prev_block(r, slot):
    sums = prefix_sums(r.aux[slot, 0:8, :])
    whole = sums[:, BLK - 1:BLK]
    doc_last = r.aux[1, 8:9, BLK - 1:BLK]
    weight = jnp.exp(whole - sums + r.tail[:, 0:1])
    r.tail[...] = r.tail[...] + whole
    r.bdec[...] = jnp.where(r.aux[slot, 8:9, :] == doc_last, weight, 0.0)
    doc_c = to_columns(r.aux[slot, 8:16, :])[:, 0:1]
    r.kmask[...] = jnp.broadcast_to(jnp.where(doc_c == doc_last, 0.0, -BIG), (BLK, 128))
    r.qoff[...] = jnp.broadcast_to(jnp.where(r.aux[0, 8:9, :] == doc_last, 0.0, -BIG), (8, BLK))
    r.xt[0:128, :] = t16(r.kvb[slot, 1])
    r.bt[...] = jnp.transpose(r.kvb[slot, 2].astype(F32))

    def score(h, qt):
        cols = slice(qt * TQ, (qt + 1) * TQ)
        return dot_nt(r.kvb[slot, 0], r.q[h, cols, :])

    def soft(h, qt, s):
        cols = slice(qt * TQ, (qt + 1) * TQ)
        km = r.kmask[...]
        s = s + jnp.concatenate([km] * (TQ // 128), axis=1)
        qoff = r.qoff[0:1, cols]
        m_old = r.m[h, 0:1, cols]
        m = jnp.maximum(m_old, fold_max(s) + qoff)
        f = jnp.exp2((m_old - m) * SC)
        p = jnp.exp2((s - (m - qoff)) * SC)
        r.m[h, :, cols] = jnp.broadcast_to(m, (8, TQ))
        r.sq[h, :, cols] = r.sq[h, :, cols] * (f * f) + fold_sum(p * p)
        r.cross[h, :, cols] = r.cross[h, :, cols] * f
        return p.astype(BF16), f

    def apply(h, qt, xt, p, f):
        cols = slice(qt * TQ, (qt + 1) * TQ)
        r.acc[h, :, cols] = r.acc[h, :, cols] * f + dot(xt, p)

    def heads(i, _):
        units = [(i * UNROLL + u, qt) for u in range(UNROLL) for qt in range(BLK // TQ)]
        xts = []
        for u in range(UNROLL):
            h = i * UNROLL + u
            xb = (r.bt[...] * r.bdec[pl.ds(h, 1), :]).astype(BF16)
            xts.append(jnp.concatenate([r.xt[0:128, :], xb, r.xt[256:XR, :]], axis=0))
            r.state[h] = r.state[h] + dot_nt(xts[u][0:256], xb)
        nxt = score(*units[0])
        prev = None
        for j, (h, qt) in enumerate(units):
            cur = nxt
            if j + 1 < len(units):
                nxt = score(*units[j + 1])
            pf = soft(h, qt, cur)
            if prev is not None:
                apply(*prev)
            prev = (h, qt, xts[j // (BLK // TQ)]) + pf
        apply(*prev)
        return 0
    lax.fori_loop(0, HG // UNROLL, heads, 0)


def finish(r, w):
    doc_last = r.aux[1, 8:9, BLK - 1:BLK]
    from_prev = jnp.where((r.aux[0, 8:9, :] == doc_last) & (w.s > 0), 1.0, 0.0)
    r.ct[...] = jnp.transpose(r.outer_own[...].astype(F32))
    r.ssq[...] = jnp.zeros((8, BLK), F32)

    def head(h, _):
        cf = r.ct[...]
        a = jnp.exp(r.csum[pl.ds(h, 1), :]) * from_prev
        y = dot_nt(r.state[h].astype(BF16), r.outer_own[...])
        inv = 1.0 / r.acc[h, 256:257, :]
        tf = r.acc[h, 0:128, :] * inv
        sf = r.stud[h] + a * y[0:128, :]
        r.teach[h] = jnp.transpose(tf).astype(BF16)
        r.student[h] = jnp.transpose(sf).astype(BF16)
        terms = (r.mixsq[h] + (a * a) * fold_sum(y[128:256, :] * cf)
                 - (2.0 * inv) * (r.cross[h] + a * fold_sum(cf * r.acc[h, 128:256, :]))
                 + (inv * inv) * r.sq[h])
        r.err[pl.ds(h, 1), :] = jnp.sum(terms, axis=0, keepdims=True)
        r.ssq[0:1, :] = r.ssq[0:1, :] + jnp.sum(fold_sum(tf * tf), axis=0, keepdims=True)
        r.ssq[1:2, :] = r.ssq[1:2, :] + jnp.sum(fold_sum(sf * sf), axis=0, keepdims=True)
        return 0
    lax.fori_loop(0, HG, head, 0)


def ssq_copy(r, w, k):
    return remote(r.ssq, r.ssq_all.at[w.g], r.ssq_send.at[k], r.ssq_recv.at[w.g], (w.s, ((w.g + k) % 8) * 2 + w.c))


def ssq_from(r, w, k):
    g = (w.g + 8 - k) % 8
    return remote(r.ssq, r.ssq_all.at[g], r.ssq_send.at[k], r.ssq_recv.at[g], (w.s, g * 2 + w.c))


def out_copy(r, w, k):
    to = (w.hd + k) % 16
    return remote(r.gap.at[pl.ds(pl.multiple_of(to * 32, 32), 32)],
                  r.out.at[w.c, :, pl.ds(pl.multiple_of(w.g * 1024, 1024), 1024)],
                  r.out_send.at[k], r.out_recv.at[w.hd], (w.s, to))


def out_from(r, w, k):
    sender = (w.hd + 16 - k) % 16
    return remote(r.gap.at[0:32],
                  r.out.at[sender % 2, :, pl.ds(pl.multiple_of((sender // 2) * 1024, 1024), 1024)],
                  r.out_send.at[k], r.out_recv.at[sender], (w.s, sender))


def share(r, w):
    for k in range(1, 8):
        ssq_copy(r, w, k).start()
    r.ssq_all[pl.ds(w.g, 1)] = r.ssq[...].reshape(1, 8, BLK)
    top, bottom = r.err[0:4, :], r.err[4:8, :]
    filler = jnp.zeros((4, BLK), F32)
    r.err_pair[0] = jnp.concatenate([jnp.where(w.c == 0, top, bottom), filler], axis=0)
    r.err_pair[1] = jnp.concatenate([jnp.where(w.c == 0, bottom, top), filler], axis=0)
    err_far = remote(r.err_pair.at[1], r.err_out.at[w.c], r.swap_send.at[2], r.swap_recv.at[2], w.sibling)
    err_far.start()
    err_near = pltpu.make_async_copy(r.err_pair.at[0], r.err_out.at[w.c], r.load_sem.at[0])
    err_near.start()
    for k in range(1, 8):
        ssq_from(r, w, k).wait_recv()
    sums = jnp.sum(r.ssq_all[...], axis=0)
    scale = lax.rsqrt(sums / (8.0 * HG * 128) + EPS)
    cols = to_columns(scale)
    t_scale, s_scale = cols[:, 0:1], cols[:, 1:2]
    gain = r.gain[pl.ds(w.g, 1), :]
    for h in range(HG):
        lanes = slice(h * 128, (h + 1) * 128)
        gap = gain[:, lanes] * r.student[h].astype(F32) * s_scale - r.teach[h].astype(F32) * t_scale
        r.gap[:, lanes] = gap.astype(BF16)
    for k in range(1, 16):
        out_copy(r, w, k).start()
    own = pltpu.make_async_copy(
        r.gap.at[pl.ds(pl.multiple_of(w.hd * 32, 32), 32)],
        r.out.at[w.c, :, pl.ds(pl.multiple_of(w.g * 1024, 1024), 1024)], r.load_sem.at[1])
    own.start()
    err_near.wait()
    own.wait()
    err_far.wait_send()
    remote(r.err_pair.at[1], r.err_out.at[1 - w.c], r.swap_send.at[2], r.swap_recv.at[2], w.sibling).wait_recv()
    for k in range(1, 16):
        out_from(r, w, k).wait_recv()
    for k in range(1, 8):
        ssq_copy(r, w, k).wait_send()
    for k in range(1, 16):
        out_copy(r, w, k).wait_send()


ARGS = ("query", "key", "value", "inner", "outer", "aux_in", "gain")
OUTS = ("out", "err_out")
DMA = pltpu.SemaphoreType.DMA
SCRATCH = dict(
    qraw=pltpu.VMEM((2, 2048, 128), BF16), aux_raw=pltpu.VMEM((2, 8, BLK), F32),
    raw=pltpu.VMEM((4, 4096, 128), BF16), wide=pltpu.VMEM((4096, 128), F32),
    q=pltpu.VMEM((HG, BLK, 128), BF16), kvb=pltpu.VMEM((SLOTS, 3, BLK, 128), BF16),
    aux=pltpu.VMEM((SLOTS, 16, BLK), F32), outer_own=pltpu.VMEM((BLK, 128), BF16),
    csum=pltpu.VMEM((8, BLK), F32), csum_col=pltpu.VMEM((BLK, 128), F32),
    cb=pltpu.VMEM((BLK, BLK), F32), hide=pltpu.VMEM((BLK, BLK), F32),
    m=pltpu.VMEM((HG, 8, BLK), F32), sq=pltpu.VMEM((HG, 8, BLK), F32),
    cross=pltpu.VMEM((HG, 8, BLK), F32), mixsq=pltpu.VMEM((HG, 8, BLK), F32),
    acc=pltpu.VMEM((HG, XR, BLK), F32), stud=pltpu.VMEM((HG, 128, BLK), F32),
    state=pltpu.VMEM((HG, 256, 128), F32), bdec=pltpu.VMEM((8, BLK), F32), tail=pltpu.VMEM((8, 128), F32),
    kmask=pltpu.VMEM((BLK, 128), F32), qoff=pltpu.VMEM((8, BLK), F32),
    xt=pltpu.VMEM((XR, BLK), BF16), vo=pltpu.VMEM((144, BLK), BF16), bt=pltpu.VMEM((128, BLK), F32),
    ct=pltpu.VMEM((128, BLK), F32),
    teach=pltpu.VMEM((HG, BLK, 128), BF16), student=pltpu.VMEM((HG, BLK, 128), BF16),
    err=pltpu.VMEM((8, BLK), F32), err_pair=pltpu.VMEM((2, 8, BLK), F32),
    ssq=pltpu.VMEM((8, BLK), F32), ssq_all=pltpu.VMEM((8, 8, BLK), F32), gap=pltpu.VMEM((BLK, HG * 128), BF16),
    load_sem=DMA((6,)), swap_send=DMA((3,)), swap_recv=DMA((3,)),
    up_send=DMA((2, 4)), up_recv=DMA((2, 4)), side_send=DMA((2, 4)), side_recv=DMA((2, 4)),
    ssq_send=DMA((8,)), ssq_recv=DMA((8,)), out_send=DMA((16,)), out_recv=DMA((16,)),
)


def kernel(*refs):
    r = Refs()
    for name, ref in zip(ARGS + OUTS + tuple(SCRATCH), refs):
        setattr(r, name, ref)
    w = Place()
    load_own(r, w)
    own_prepare(r)
    own_block(r)

    @pl.when(w.s == 0)
    def _():
        r.aux[1] = jnp.zeros((16, BLK), F32)
    take_up(r, w, 0)
    take_side(r, w, 0)

    def earlier(slot, _):
        prev_block(r, slot)
        return 0
    lax.fori_loop(1, jnp.minimum(w.s, 2) + 1, earlier, 0)
    take_up(r, w, 1)
    take_side(r, w, 1)
    lax.fori_loop(3, jnp.minimum(w.s, 4) + 1, earlier, 0)
    finish(r, w)
    share(r, w)
    end_sends(r, w)


def on_device(query_rows, key_rows, value_rows, state_in, state_out, log_decay, doc_ids, norm_gain):
    docs = jnp.broadcast_to(doc_ids.astype(F32)[:, None, :], (2, 4, BLK))
    aux_in = jnp.concatenate([log_decay, docs], axis=1)
    flat = [x.reshape(2, -1, 128) for x in (query_rows, key_rows, value_rows, state_in, state_out)]
    out, err = pl.pallas_call(
        kernel,
        out_shape=(jax.ShapeDtypeStruct((2, 32, 8192), BF16), jax.ShapeDtypeStruct((2, 8, BLK), F32)),
        in_specs=[pl.BlockSpec(memory_space=pl.ANY)] * 6 + [pl.BlockSpec(memory_space=pltpu.VMEM)],
        out_specs=(pl.BlockSpec(memory_space=pl.ANY), pl.BlockSpec(memory_space=pl.ANY)),
        scratch_shapes=list(SCRATCH.values()),
        compiler_params=pltpu.CompilerParams(collective_id=0, has_side_effects=True, vmem_limit_bytes=56 * 2**20),
        cost_estimate=pl.CostEstimate(flops=10**10, bytes_accessed=10**7, transcendentals=0),
    )(*flat, aux_in, norm_gain.reshape(8, 1024))
    return (out, err[:, 0:4, :])


def solution(mesh):
    placed = (
        P(None, "seq", "head", None),
        P(None, "seq", None, None),
        P(None, "seq", None, None),
        P(None, "seq", None, None),
        P(None, "seq", None, None),
        P(None, "head", "seq"),
        P(None, "seq"),
        P(),
    )
    return jax.shard_map(
        on_device,
        mesh=mesh,
        in_specs=placed,
        out_specs=(P(None, ("seq", "head"), None), P(None, "head", "seq")),
        check_vma=False,
    )
```

```python
import math

import jax
import jax.numpy as jnp
from jax import lax
from jax.experimental import pallas as pl
from jax.experimental.pallas import tpu as pltpu
from jax.sharding import PartitionSpec as P

F32, BF16 = jnp.float32, jnp.bfloat16
BLK, HG, SLOTS, TQ = 512, 8, 5, 256
UNROLL = 2
XR = 272
LOG2E = 1.4426950408889634
SC = LOG2E / math.sqrt(128.0)
BIG = 1e30
EPS = 1e-05
NT = (((1,), (1,)), ((), ()))
MESH = pl.DeviceIdType.MESH


def dot_nt(a, b):
    return lax.dot_general(a, b, NT, preferred_element_type=F32)


def dot(a, b):
    return jnp.dot(a, b, preferred_element_type=F32)


def fold_sum(x):
    return jnp.sum(x.reshape(x.shape[0] // 8, 8, x.shape[1]), axis=0)


def fold_max(x):
    return jnp.max(jnp.max(x.reshape(x.shape[0] // 8, 8, x.shape[1]), axis=0), axis=0, keepdims=True)


def prefix_sums(x):
    lane = lax.broadcasted_iota(jnp.int32, x.shape, 1)
    step = 1
    while step < x.shape[1]:
        x = x + jnp.where(lane >= step, pltpu.roll(x, step, 1), 0.0)
        step *= 2
    return x


def to_columns(rows):
    wide = jnp.concatenate([rows, jnp.zeros((120, rows.shape[1]), F32)], axis=0)
    return jnp.transpose(wide)


def t16(x):
    return jnp.transpose(x.astype(F32)).astype(BF16)


class Refs:
    pass


class Place:
    def __init__(self):
        self.s, self.hd = lax.axis_index("seq"), lax.axis_index("head")
        self.z, self.col = self.s // 2, self.s % 2
        self.g, self.c = self.hd // 2, self.hd % 2
        self.sibling = (self.s, self.g * 2 + 1 - self.c)
        self.beside = (self.z * 2 + 1 - self.col, self.hd)
        self.above = (self.s + 2, self.hd)
        self.below = (self.s - 2, self.hd)


def remote(src, dst, send, recv, device):
    return pltpu.make_async_remote_copy(
        src_ref=src, dst_ref=dst, send_sem=send, recv_sem=recv, device_id=device, device_id_type=MESH)


def greet(w):
    barrier = pltpu.get_barrier_semaphore()

    def tell(device):
        pl.semaphore_signal(barrier, inc=1, device_id=device, device_id_type=MESH)

    def others(k, _):
        tell((w.s, (w.hd + k) % 16))
        return 0
    lax.fori_loop(1, 16, others, 0)
    tell(w.beside)

    @pl.when(w.z < 3)
    def _():
        tell(w.above)

    @pl.when(w.z > 0)
    def _():
        tell(w.below)
    pl.semaphore_wait(barrier, 16 + (w.z + 2) // 3 + (5 - w.z) // 3 - 0)


def swap_copies(r, w):
    return (remote(r.query.at[1 - w.c], r.qraw.at[1], r.swap_send.at[0], r.swap_recv.at[0], w.sibling),
            remote(r.decay.at[1 - w.c], r.decay_raw.at[1], r.swap_send.at[1], r.swap_recv.at[1], w.sibling))


def part(r, slot, j):
    return r.aux.at[slot] if j == 3 else r.kvb.at[slot, j]


def up_copy(r, w, step, j):
    return remote(part(r, 2 * step, j), part(r, 2 * step + 2, j), r.up_send.at[step, j], r.up_recv.at[step, j], w.above)


def side_copy(r, w, step, j):
    return remote(part(r, 2 * step + 2 * w.col, j), part(r, 2 * step + 1, j), r.side_send.at[step, j], r.side_recv.at[step, j], w.beside)


def sends_up(w, step):
    return (w.z < 3) if step == 0 else ((w.z >= 1) & (w.z < 3))


def sends_side(w, step):
    return w.z >= step + w.col


def gets_up(w, step):
    return w.z >= step + 1


def gets_side(w, step):
    return w.z >= step + 1 - w.col


def load_own(r, w):
    loads = [pltpu.make_async_copy(ref.at[w.c], r.raw.at[i], r.load_sem.at[i])
             for i, ref in enumerate((r.key, r.value, r.inner, r.outer))]
    qload = pltpu.make_async_copy(r.query.at[w.c], r.qraw.at[0], r.load_sem.at[4])
    aload = pltpu.make_async_copy(r.decay.at[w.c], r.decay_raw.at[0], r.load_sem.at[5])
    aload.start()
    for x in loads:
        x.start()
    qload.start()
    greet(w)
    swaps = swap_copies(r, w)
    swaps[1].start()
    swaps[0].start()

    def send_part(j):
        @pl.when(sends_up(w, 0))
        def _():
            up_copy(r, w, 0, j).start()

        @pl.when((w.col == 0) & sends_side(w, 0))
        def _():
            side_copy(r, w, 0, j).start()

    aload.wait()
    swaps[1].wait_recv()
    mine, theirs = r.decay_raw[0], r.decay_raw[1]
    first = jnp.where(w.c == 0, mine, theirs)
    second = jnp.where(w.c == 0, theirs, mine)
    r.aux[0, 0:8, :] = jnp.concatenate([first, second], axis=0)
    docs = jnp.where(w.c == 0, r.docs[0:1, :], r.docs[1:2, :]).astype(F32)
    r.aux[0, 8:16, :] = jnp.broadcast_to(docs, (8, BLK))
    send_part(3)
    for i in range(4):
        loads[i].wait()
        r.wide[...] = r.raw[i].astype(F32)
        rows = r.wide[pl.ds(w.g, BLK, stride=8), :].astype(BF16)
        if i < 3:
            r.kvb[0, i] = rows
            send_part(i)
        else:
            r.outer_own[...] = rows
    qload.wait()
    swaps[0].wait_recv()
    for i in range(2):
        r.wide[0:2048, :] = r.qraw[i].astype(F32)
        base = 4 * w.c if i == 0 else 4 - 4 * w.c
        for j in range(4):
            r.q[base + j] = r.wide[pl.ds(j, BLK, stride=4), :].astype(BF16)
    for x in swaps:
        x.wait_send()


def take_up(r, w, step, parts):
    @pl.when(gets_up(w, step))
    def _():
        for j in parts:
            up_copy(r, w, step, j).wait_recv()
            if step == 0:
                @pl.when(sends_up(w, 1))
                def _():
                    up_copy(r, w, 1, j).start()

                side_copy(r, w, 1 - w.col, j).start()
            else:
                @pl.when(w.col == 1)
                def _():
                    side_copy(r, w, 1, j).start()


def take_side(r, w, step, parts):
    for j in parts:
        side_copy(r, w, step, j).wait_recv()


def end_sends(r, w):
    for step in range(2):
        @pl.when(sends_up(w, step))
        def _():
            for j in range(4):
                up_copy(r, w, step, j).wait_send()

        @pl.when(sends_side(w, step))
        def _():
            for j in range(4):
                side_copy(r, w, step, j).wait_send()


def own_prepare(r):
    own = prefix_sums(r.aux[0, 0:8, :])
    r.csum[...] = own
    r.csum_col[...] = to_columns(own)
    doc_c = to_columns(r.aux[0, 8:16, :])[:, 0:1]
    cb = dot_nt(r.kvb[0, 2], r.outer_own[...])
    kj = lax.broadcasted_iota(jnp.int32, (BLK, BLK), 0)
    qi = lax.broadcasted_iota(jnp.int32, (BLK, BLK), 1)
    seen = (qi >= kj) & (doc_c == r.aux[0, 8:9, :])
    r.cb[...] = jnp.where(seen, cb, 0.0)
    r.hide[...] = jnp.where(seen, 0.0, -BIG)
    r.xt[0:128, :] = t16(r.kvb[0, 1])
    r.xt[256:XR, :] = jnp.ones((XR - 256, BLK), BF16)
    r.vo[0:128, :] = r.xt[0:128, :]
    r.vo[128:144, :] = jnp.ones((16, BLK), BF16)


def own_block(r, start, stop):
    def head(h, _):
        lanes = lax.broadcasted_iota(jnp.int32, (BLK, 128), 1)
        acol = jnp.sum(jnp.where(lanes == h, r.csum_col[...], 0.0), axis=1, keepdims=True)
        arow = r.csum[pl.ds(h, 1), :]
        for qt in range(BLK // TQ):
            cols = slice(qt * TQ, (qt + 1) * TQ)
            n = (qt + 1) * TQ
            s = dot_nt(r.kvb[0, 0, 0:n, :], r.q[h, cols, :]) + r.hide[0:n, cols]
            m = fold_max(s)
            p = jnp.exp2((s - m) * SC)
            mix = jnp.exp2(jnp.minimum((arow[:, cols] - acol[0:n]) * LOG2E, 0.0)) * r.cb[0:n, cols]
            av = dot(r.vo[:, 0:n], p.astype(BF16))
            r.m[h, :, cols] = jnp.broadcast_to(m, (8, TQ))
            r.sq[h, :, cols] = fold_sum(p * p)
            r.cross[h, :, cols] = fold_sum(p * mix)
            r.mixsq[h, :, cols] = fold_sum(mix * mix)
            r.acc[h, 0:128, cols] = av[0:128]
            r.acc[h, 128:256, cols] = jnp.zeros((128, TQ), F32)
            r.acc[h, 256:XR, cols] = av[128:144]
            r.stud[h, :, cols] = dot(r.vo[0:128, 0:n], mix.astype(BF16))
        r.state[h] = jnp.zeros((256, 128), F32)
        return 0
    lax.fori_loop(start, stop, head, 0)


def prev_block(r, w, slot, between=None):
    sums = prefix_sums(r.aux[slot, 0:8, :])
    whole = sums[:, BLK - 1:BLK]
    doc_last = r.aux[1, 8:9, BLK - 1:BLK]
    tail = jnp.zeros((8, 1), F32)
    for t in range(1, slot):
        tail = tail + jnp.sum(r.aux[t, 0:8, :], axis=1, keepdims=True)
    weight = jnp.exp(whole - sums + tail)
    r.bdec[...] = jnp.where(r.aux[slot, 8:9, :] == doc_last, weight, 0.0)
    doc_c = to_columns(r.aux[slot, 8:16, :])[:, 0:1]
    r.kmask[...] = jnp.broadcast_to(jnp.where(doc_c == doc_last, 0.0, -BIG), (BLK, 128))
    r.qoff[...] = jnp.broadcast_to(jnp.where(r.aux[0, 8:9, :] == doc_last, 0.0, -BIG), (8, BLK))
    r.xt[0:128, :] = t16(r.kvb[slot, 1])
    r.bt[...] = jnp.transpose(r.kvb[slot, 2].astype(F32))

    def score(h, qt):
        cols = slice(qt * TQ, (qt + 1) * TQ)
        return dot_nt(r.kvb[slot, 0], r.q[h, cols, :])

    def soft(h, qt, s):
        cols = slice(qt * TQ, (qt + 1) * TQ)
        km = r.kmask[...]
        s = s + jnp.concatenate([km] * (TQ // 128), axis=1)
        qoff = r.qoff[0:1, cols]
        m_old = r.m[h, 0:1, cols]
        m = jnp.maximum(m_old, fold_max(s) + qoff)
        f = jnp.exp2((m_old - m) * SC)
        p = jnp.exp2((s - (m - qoff)) * SC)
        r.m[h, :, cols] = jnp.broadcast_to(m, (8, TQ))
        r.sq[h, :, cols] = r.sq[h, :, cols] * (f * f) + fold_sum(p * p)
        r.cross[h, :, cols] = r.cross[h, :, cols] * f
        return p.astype(BF16), f

    def apply(h, qt, xt, p, f):
        cols = slice(qt * TQ, (qt + 1) * TQ)
        r.acc[h, :, cols] = r.acc[h, :, cols] * f + dot(xt, p)

    def heads(i, _):
        units = [(i * UNROLL + u, qt) for u in range(UNROLL) for qt in range(BLK // TQ)]
        xts = []
        for u in range(UNROLL):
            h = i * UNROLL + u
            xb = (r.bt[...] * r.bdec[pl.ds(h, 1), :]).astype(BF16)
            xts.append(jnp.concatenate([r.xt[0:128, :], xb, r.xt[256:XR, :]], axis=0))
            r.state[h] = r.state[h] + dot_nt(xts[u][0:256], xb)
        nxt = score(*units[0])
        prev = None
        for j, (h, qt) in enumerate(units):
            cur = nxt
            if j + 1 < len(units):
                nxt = score(*units[j + 1])
            pf = soft(h, qt, cur)
            if prev is not None:
                apply(*prev)
            prev = (h, qt, xts[j // (BLK // TQ)]) + pf
        apply(*prev)
        return 0
    half = HG // UNROLL // 2
    lax.fori_loop(0, half, heads, 0)
    if between is not None:
        between()
    lax.fori_loop(half, 2 * half, heads, 0)


def finish(r, w):
    doc_last = r.aux[1, 8:9, BLK - 1:BLK]
    from_prev = jnp.where((r.aux[0, 8:9, :] == doc_last) & (w.s > 0), 1.0, 0.0)
    r.ct[...] = jnp.transpose(r.outer_own[...].astype(F32))
    r.ssq[...] = jnp.zeros((8, BLK), F32)

    def head(h, _):
        cf = r.ct[...]
        a = jnp.exp(r.csum[pl.ds(h, 1), :]) * from_prev
        y = dot_nt(r.state[h].astype(BF16), r.outer_own[...])
        inv = 1.0 / r.acc[h, 256:257, :]
        tf = r.acc[h, 0:128, :] * inv
        sf = r.stud[h] + a * y[0:128, :]
        r.teach[h] = jnp.transpose(tf).astype(BF16)
        r.student[h] = jnp.transpose(sf).astype(BF16)
        terms = (r.mixsq[h] + (a * a) * fold_sum(y[128:256, :] * cf)
                 - (2.0 * inv) * (r.cross[h] + a * fold_sum(cf * r.acc[h, 128:256, :]))
                 + (inv * inv) * r.sq[h])
        r.err[pl.ds(h, 1), :] = jnp.sum(terms, axis=0, keepdims=True)
        r.ssq[0:1, :] = r.ssq[0:1, :] + jnp.sum(fold_sum(tf * tf), axis=0, keepdims=True)
        r.ssq[1:2, :] = r.ssq[1:2, :] + jnp.sum(fold_sum(sf * sf), axis=0, keepdims=True)
        return 0
    lax.fori_loop(0, HG, head, 0)


def ssq_copy(r, w, k):
    return remote(r.ssq, r.ssq_all.at[w.g], r.ssq_send.at[k], r.ssq_recv.at[w.g], (w.s, ((w.g + k) % 8) * 2 + w.c))


def ssq_from(r, w, k):
    g = (w.g + 8 - k) % 8
    return remote(r.ssq, r.ssq_all.at[g], r.ssq_send.at[k], r.ssq_recv.at[g], (w.s, g * 2 + w.c))


def out_copy(r, w, k):
    to = (w.hd + k) % 16
    return remote(r.gap.at[pl.ds(pl.multiple_of(to * 32, 32), 32)],
                  r.out.at[w.c, :, pl.ds(pl.multiple_of(w.g * 1024, 1024), 1024)],
                  r.out_send.at[k], r.out_recv.at[w.hd], (w.s, to))


def out_from(r, w, k):
    sender = (w.hd + 16 - k) % 16
    return remote(r.gap.at[0:32],
                  r.out.at[sender % 2, :, pl.ds(pl.multiple_of((sender // 2) * 1024, 1024), 1024)],
                  r.out_send.at[k], r.out_recv.at[sender], (w.s, sender))


def share(r, w):
    for k in range(1, 8):
        ssq_copy(r, w, k).start()
    r.ssq_all[pl.ds(w.g, 1)] = r.ssq[...].reshape(1, 8, BLK)
    top, bottom = r.err[0:4, :], r.err[4:8, :]
    r.err_pair[0] = jnp.where(w.c == 0, top, bottom)
    r.err_pair[1] = jnp.where(w.c == 0, bottom, top)
    err_far = remote(r.err_pair.at[1], r.err_out.at[w.c], r.swap_send.at[2], r.swap_recv.at[2], w.sibling)
    err_far.start()
    err_near = pltpu.make_async_copy(r.err_pair.at[0], r.err_out.at[w.c], r.load_sem.at[0])
    err_near.start()
    for k in range(1, 8):
        ssq_from(r, w, k).wait_recv()
    sums = jnp.sum(r.ssq_all[...], axis=0)
    scale = lax.rsqrt(sums / (8.0 * HG * 128) + EPS)
    cols = to_columns(scale)
    t_scale, s_scale = cols[:, 0:1], cols[:, 1:2]
    gain = r.gain[pl.ds(pl.multiple_of(w.g * 1024, 1024), 1024)].reshape(1, 1024)
    for h in range(HG):
        lanes = slice(h * 128, (h + 1) * 128)
        gap = gain[:, lanes] * r.student[h].astype(F32) * s_scale - r.teach[h].astype(F32) * t_scale
        r.gap[:, lanes] = gap.astype(BF16)
    for k in range(1, 16):
        out_copy(r, w, k).start()
    own = pltpu.make_async_copy(
        r.gap.at[pl.ds(pl.multiple_of(w.hd * 32, 32), 32)],
        r.out.at[w.c, :, pl.ds(pl.multiple_of(w.g * 1024, 1024), 1024)], r.load_sem.at[1])
    own.start()
    err_near.wait()
    own.wait()
    err_far.wait_send()
    remote(r.err_pair.at[1], r.err_out.at[1 - w.c], r.swap_send.at[2], r.swap_recv.at[2], w.sibling).wait_recv()
    for k in range(1, 16):
        out_from(r, w, k).wait_recv()
    for k in range(1, 8):
        ssq_copy(r, w, k).wait_send()
    for k in range(1, 16):
        out_copy(r, w, k).wait_send()


ARGS = ("query", "key", "value", "inner", "outer", "decay", "docs", "gain")
OUTS = ("out", "err_out")
DMA = pltpu.SemaphoreType.DMA
SCRATCH = dict(
    qraw=pltpu.VMEM((2, 2048, 128), BF16), decay_raw=pltpu.VMEM((2, 4, BLK), F32),
    raw=pltpu.VMEM((4, 4096, 128), BF16), wide=pltpu.VMEM((4096, 128), F32),
    q=pltpu.VMEM((HG, BLK, 128), BF16), kvb=pltpu.VMEM((SLOTS, 3, BLK, 128), BF16),
    aux=pltpu.VMEM((SLOTS, 16, BLK), F32), outer_own=pltpu.VMEM((BLK, 128), BF16),
    csum=pltpu.VMEM((8, BLK), F32), csum_col=pltpu.VMEM((BLK, 128), F32),
    cb=pltpu.VMEM((BLK, BLK), F32), hide=pltpu.VMEM((BLK, BLK), F32),
    m=pltpu.VMEM((HG, 8, BLK), F32), sq=pltpu.VMEM((HG, 8, BLK), F32),
    cross=pltpu.VMEM((HG, 8, BLK), F32), mixsq=pltpu.VMEM((HG, 8, BLK), F32),
    acc=pltpu.VMEM((HG, XR, BLK), F32), stud=pltpu.VMEM((HG, 128, BLK), F32),
    state=pltpu.VMEM((HG, 256, 128), F32), bdec=pltpu.VMEM((8, BLK), F32),
    kmask=pltpu.VMEM((BLK, 128), F32), qoff=pltpu.VMEM((8, BLK), F32),
    xt=pltpu.VMEM((XR, BLK), BF16), vo=pltpu.VMEM((144, BLK), BF16), bt=pltpu.VMEM((128, BLK), F32),
    ct=pltpu.VMEM((128, BLK), F32),
    teach=pltpu.VMEM((HG, BLK, 128), BF16), student=pltpu.VMEM((HG, BLK, 128), BF16),
    err=pltpu.VMEM((8, BLK), F32), err_pair=pltpu.VMEM((2, 4, BLK), F32),
    ssq=pltpu.VMEM((8, BLK), F32), ssq_all=pltpu.VMEM((8, 8, BLK), F32), gap=pltpu.VMEM((BLK, HG * 128), BF16),
    load_sem=DMA((6,)), swap_send=DMA((3,)), swap_recv=DMA((3,)),
    up_send=DMA((2, 4)), up_recv=DMA((2, 4)), side_send=DMA((2, 4)), side_recv=DMA((2, 4)),
    ssq_send=DMA((8,)), ssq_recv=DMA((8,)), out_send=DMA((16,)), out_recv=DMA((16,)),
)


def kernel(*refs):
    r = Refs()
    for name, ref in zip(ARGS + OUTS + tuple(SCRATCH), refs):
        setattr(r, name, ref)
    w = Place()
    load_own(r, w)
    own_prepare(r)
    own_block(r, 0, 4)
    take_up(r, w, 0, (3, 0))
    own_block(r, 4, 8)
    take_up(r, w, 0, (1, 2))

    @pl.when(w.s == 0)
    def _():
        r.aux[1] = jnp.zeros((16, BLK), F32)

    @pl.when(gets_side(w, 0))
    def _():
        side_copy(r, w, 0, 3).wait_recv()

    @pl.when(w.s >= 2)
    def _():
        prev_block(r, w, 2, lambda: take_up(r, w, 1, (3, 0)))
        take_up(r, w, 1, (1, 2))

    @pl.when(w.s >= 1)
    def _():
        take_side(r, w, 0, (0, 1, 2))
        prev_block(r, w, 1)

    @pl.when(w.s >= 4)
    def _():
        take_side(r, w, 1, (3,))
        prev_block(r, w, 4)

    @pl.when(w.s == 3)
    def _():
        take_side(r, w, 1, (3,))

    @pl.when(w.s >= 3)
    def _():
        take_side(r, w, 1, (0, 1, 2))
        prev_block(r, w, 3)
    finish(r, w)
    share(r, w)
    end_sends(r, w)


def on_device(query_rows, key_rows, value_rows, state_in, state_out, log_decay, doc_ids, norm_gain):
    flat = [x.reshape(2, -1, 128) for x in (query_rows, key_rows, value_rows, state_in, state_out)]
    return pl.pallas_call(
        kernel,
        out_shape=(jax.ShapeDtypeStruct((2, 32, 8192), BF16), jax.ShapeDtypeStruct((2, 4, BLK), F32)),
        in_specs=[pl.BlockSpec(memory_space=pl.ANY)] * 6 + [pl.BlockSpec(memory_space=pltpu.VMEM)] * 2,
        out_specs=(pl.BlockSpec(memory_space=pl.ANY), pl.BlockSpec(memory_space=pl.ANY)),
        scratch_shapes=list(SCRATCH.values()),
        compiler_params=pltpu.CompilerParams(collective_id=0, has_side_effects=True, vmem_limit_bytes=56 * 2**20),
        cost_estimate=pl.CostEstimate(flops=10**10, bytes_accessed=10**7, transcendentals=0),
    )(*flat, log_decay, doc_ids, norm_gain)


def solution(mesh):
    placed = (
        P(None, "seq", "head", None),
        P(None, "seq", None, None),
        P(None, "seq", None, None),
        P(None, "seq", None, None),
        P(None, "seq", None, None),
        P(None, "head", "seq"),
        P(None, "seq"),
        P(),
    )
    return jax.shard_map(
        on_device,
        mesh=mesh,
        in_specs=placed,
        out_specs=(P(None, ("seq", "head"), None), P(None, "head", "seq")),
        check_vma=False,
    )
```

```python
import math

import jax
import jax.numpy as jnp
from jax import lax
from jax.experimental import pallas as pl
from jax.experimental.pallas import tpu as pltpu
from jax.sharding import PartitionSpec as P

F32, BF16 = jnp.float32, jnp.bfloat16
BLK, HG, SLOTS, TQ = 512, 8, 5, 256
XR = 272
LOG2E = 1.4426950408889634
SC = LOG2E / math.sqrt(128.0)
BIG = 1e30
EPS = 1e-05
NT = (((1,), (1,)), ((), ()))
MESH = pl.DeviceIdType.MESH


def dot_nt(a, b):
    return lax.dot_general(a, b, NT, preferred_element_type=F32)


def dot(a, b):
    return jnp.dot(a, b, preferred_element_type=F32)


def fold_sum(x):
    return jnp.sum(x.reshape(x.shape[0] // 8, 8, x.shape[1]), axis=0)


def fold_max(x):
    return jnp.max(jnp.max(x.reshape(x.shape[0] // 8, 8, x.shape[1]), axis=0), axis=0, keepdims=True)


def prefix_sums(x):
    lane = lax.broadcasted_iota(jnp.int32, x.shape, 1)
    step = 1
    while step < x.shape[1]:
        x = x + jnp.where(lane >= step, pltpu.roll(x, step, 1), 0.0)
        step *= 2
    return x


def to_columns(rows):
    wide = jnp.concatenate([rows, jnp.zeros((128 - rows.shape[0], rows.shape[1]), F32)], axis=0)
    return jnp.transpose(wide)


def t16(x):
    return jnp.transpose(x.astype(F32)).astype(BF16)


class Refs:
    pass


class Place:
    def __init__(self):
        self.s, self.hd = lax.axis_index("seq"), lax.axis_index("head")
        self.z, self.col = self.s // 2, self.s % 2
        self.g, self.c = self.hd // 2, self.hd % 2
        self.sibling = (self.s, self.g * 2 + 1 - self.c)
        self.beside = (self.z * 2 + 1 - self.col, self.hd)
        self.above = (self.s + 2, self.hd)
        self.below = (self.s - 2, self.hd)


def remote(src, dst, send, recv, device):
    return pltpu.make_async_remote_copy(
        src_ref=src, dst_ref=dst, send_sem=send, recv_sem=recv, device_id=device, device_id_type=MESH)


def greet(w):
    barrier = pltpu.get_barrier_semaphore()

    def tell(device):
        pl.semaphore_signal(barrier, inc=1, device_id=device, device_id_type=MESH)

    def others(k, _):
        tell((w.s, (w.hd + k) % 16))
        return 0
    lax.fori_loop(1, 16, others, 0)
    tell(w.beside)

    @pl.when(w.z < 3)
    def _():
        tell(w.above)

    @pl.when(w.z > 0)
    def _():
        tell(w.below)
    pl.semaphore_wait(barrier, 16 + (w.z + 2) // 3 + (5 - w.z) // 3 - 0)


def swap_copies(r, w):
    return (remote(r.query.at[1 - w.c], r.qraw.at[1], r.swap_send.at[0], r.swap_recv.at[0], w.sibling),
            remote(r.decay.at[1 - w.c], r.decay_raw.at[1], r.swap_send.at[1], r.swap_recv.at[1], w.sibling))


def spread(p):
    return (p % 256) // 32 * 64 + p // 256 * 32 + p % 32


CHUNKS = [(spread(32 * i), 32 * i) for i in range(16)]


def part(r, slot, j):
    return r.aux.at[slot] if j == 3 else r.kvb.at[slot, j]


def up_copy(r, w, step, j):
    return remote(part(r, 2 * step, j), part(r, 2 * step + 2, j), r.up_send.at[step, j], r.up_recv.at[step, j], w.above)


def side_copy(r, w, step, j):
    return remote(part(r, 2 * step + 2 * w.col, j), part(r, 2 * step + 1, j), r.side_send.at[step, j], r.side_recv.at[step, j], w.beside)


def sends_up(w, step):
    return (w.z < 3) if step == 0 else ((w.z >= 1) & (w.z < 3))


def sends_side(w, step):
    return w.z >= step + w.col


def gets_up(w, step):
    return w.z >= step + 1


def gets_side(w, step):
    return w.z >= step + 1 - w.col


def load_own(r, w):
    loads = [pltpu.make_async_copy(ref.at[w.c], r.raw.at[i], r.load_sem.at[i])
             for i, ref in enumerate((r.key, r.value, r.inner, r.outer))]
    qload = pltpu.make_async_copy(r.query.at[w.c], r.qraw.at[0], r.load_sem.at[4])
    aload = pltpu.make_async_copy(r.decay.at[w.c], r.decay_raw.at[0], r.load_sem.at[5])
    aload.start()
    for x in loads:
        x.start()
    qload.start()
    greet(w)
    swaps = swap_copies(r, w)
    swaps[1].start()
    swaps[0].start()

    def send_part(j):
        @pl.when(sends_up(w, 0))
        def _():
            up_copy(r, w, 0, j).start()

        @pl.when((w.col == 0) & sends_side(w, 0))
        def _():
            side_copy(r, w, 0, j).start()

    for i in range(4):
        loads[i].wait()
        r.wide[...] = r.raw[i].astype(F32)
        if i < 3:
            r.kvb[0, i] = r.wide[pl.ds(w.g, BLK, stride=8), :].astype(BF16)
            send_part(i)
        else:
            for pos, to in CHUNKS:
                r.outer_own[to:to + 32, :] = r.wide[pl.ds(w.g + 8 * pos, 32, stride=8), :].astype(BF16)
    aload.wait()
    swaps[1].wait_recv()
    mine, theirs = r.decay_raw[0], r.decay_raw[1]
    first = jnp.where(w.c == 0, mine, theirs)
    second = jnp.where(w.c == 0, theirs, mine)
    r.aux[0, 0:8, :] = jnp.concatenate([first, second], axis=0)
    docs = jnp.where(w.c == 0, r.docs[0:1, :], r.docs[1:2, :]).astype(F32)
    r.aux[0, 8:16, :] = jnp.broadcast_to(docs, (8, BLK))
    send_part(3)
    qload.wait()
    swaps[0].wait_recv()
    for i in range(2):
        r.wide[0:2048, :] = r.qraw[i].astype(F32)
        base = 4 * w.c if i == 0 else 4 - 4 * w.c
        for j in range(4):
            for pos, to in CHUNKS:
                r.q[base + j, to:to + 32, :] = r.wide[pl.ds(j + 4 * pos, 32, stride=4), :].astype(BF16)
    for x in swaps:
        x.wait_send()


def take_up(r, w, step, parts):
    @pl.when(gets_up(w, step))
    def _():
        for j in parts:
            up_copy(r, w, step, j).wait_recv()
            if step == 0:
                @pl.when(sends_up(w, 1))
                def _():
                    up_copy(r, w, 1, j).start()

                side_copy(r, w, 1 - w.col, j).start()
            else:
                @pl.when(w.col == 1)
                def _():
                    side_copy(r, w, 1, j).start()


def take_side(r, w, step, parts):
    for j in parts:
        side_copy(r, w, step, j).wait_recv()


def end_sends(r, w):
    for step in range(2):
        @pl.when(sends_up(w, step))
        def _():
            for j in range(4):
                up_copy(r, w, step, j).wait_send()

        @pl.when(sends_side(w, step))
        def _():
            for j in range(4):
                side_copy(r, w, step, j).wait_send()


def own_prepare(r):
    own = prefix_sums(r.aux[0, 0:8, :]) * LOG2E
    cols = to_columns(jnp.concatenate([own, r.aux[0, 8:16, :]], axis=0))
    r.csum_col[...] = cols
    rows = jnp.transpose(jnp.concatenate([cols[pos:pos + 32] for pos, _ in CHUNKS], axis=0))
    r.csum[...] = rows[0:8]
    r.docq[...] = rows[8:16]
    doc_c = cols[:, 8:9]
    cb = dot_nt(r.kvb[0, 2], r.outer_own[...])
    kj = lax.broadcasted_iota(jnp.int32, (BLK, BLK), 0)
    qi = spread(lax.broadcasted_iota(jnp.int32, (BLK, BLK), 1))
    seen = (qi >= kj) & (doc_c == r.docq[0:1, :])
    r.cb[...] = jnp.where(seen, cb, 0.0)
    r.hide[...] = jnp.where(seen, 0.0, -BIG)
    for slot in range(SLOTS):
        r.vt[slot, 128:144, :] = jnp.ones((16, BLK), BF16)
    r.vt[0, 0:128, :] = t16(r.kvb[0, 1])


def late(x):
    return jnp.concatenate([jnp.zeros_like(x), x], axis=1)


def own_half(r, qt, polls=()):
    base = qt * TQ
    parts = ((slice(0, 256), slice(0, 256)), (slice(256, 512), slice(128, 256)))
    cols = slice(base, base + TQ)
    polls = dict(polls)
    for at in range(2):
        r.pbuf[at, 256:512, 0:128] = jnp.zeros((256, 128), BF16)
        r.mbuf[at, 256:512, 0:128] = jnp.zeros((256, 128), BF16)

    def score(h):
        tops = []
        for keys, part_cols in parts:
            here = slice(base + part_cols.start, base + part_cols.stop)
            s = dot_nt(r.kvb[0, 0, keys, :], r.q[h, here, :]) + r.hide[keys, here]
            r.sbuf[h % 2, keys, part_cols] = s
            tops.append(jnp.max(s.reshape(32, 8, s.shape[1]), axis=0))
        both = jnp.concatenate([tops[0][:, 0:128], jnp.maximum(tops[0][:, 128:256], tops[1])], axis=1)
        return jnp.max(both, axis=0, keepdims=True)

    def soft(h, m):
        r.m[h, :, cols] = jnp.broadcast_to(m, (8, TQ))
        sums = []
        for keys, part_cols in parts:
            here = slice(base + part_cols.start, base + part_cols.stop)
            p = jnp.exp2((r.sbuf[h % 2, keys, part_cols] - m[:, part_cols]) * SC)
            fall = jnp.minimum(r.csum[h:h + 1, here] - r.csum_col[keys, h:h + 1], 0.0)
            mix = jnp.exp2(fall) * r.cb[keys, here]
            sums.append((fold_sum(p * p), fold_sum(p * mix), fold_sum(mix * mix)))
            r.pbuf[h % 2, keys, part_cols] = p.astype(BF16)
            r.mbuf[h % 2, keys, part_cols] = mix.astype(BF16)
        r.sq[h, :, cols], r.cross[h, :, cols], r.mixsq[h, :, cols] = (x + late(y) for x, y in zip(*sums))

    def apply(h):
        r.acc[h, 0:144, cols] = dot(r.vt[0], r.pbuf[h % 2])
        r.acc[h, 144:XR, cols] = jnp.zeros((128, TQ), F32)
        r.stud[h, :, cols] = dot(r.vt[0, 0:128, :], r.mbuf[h % 2])
        if qt == 0:
            r.state[h] = jnp.zeros((256, 128), F32)

    top = score(0)
    for h in range(HG):
        now = top
        if h + 1 < HG:
            top = score(h + 1)
        soft(h, now)
        if h > 0:
            apply(h - 1)
        if h in polls:
            polls[h]()
    apply(HG - 1)


def prepare(r, slot):
    sums = prefix_sums(r.aux[slot, 0:8, :])
    whole = sums[:, BLK - 1:BLK]
    doc_last = r.aux[1, 8:9, BLK - 1:BLK]
    tail = jnp.zeros((8, 1), F32)
    for t in range(1, slot):
        tail = tail + jnp.sum(r.aux[t, 0:8, :], axis=1, keepdims=True)
    weight = jnp.exp(whole - sums + tail)
    r.bdec[...] = jnp.where(r.aux[slot, 8:9, :] == doc_last, weight, 0.0)
    doc_c = to_columns(r.aux[slot, 8:16, :])[:, 0:1]
    r.kmask[slot] = jnp.broadcast_to(jnp.where(doc_c == doc_last, 0.0, -BIG), (BLK, 128))
    r.qoff[...] = jnp.broadcast_to(jnp.where(r.docq[0:1, :] == doc_last, 0.0, -BIG), (8, BLK))
    r.vt[slot, 0:128, :] = t16(r.kvb[slot, 1])
    r.bt[...] = jnp.transpose(r.kvb[slot, 2].astype(F32))


def slot_half(r, slot, qt, first, polls=()):
    cols = slice(qt * TQ, (qt + 1) * TQ)

    def score(h):
        mx = None
        for c in range(2):
            keys = slice(c * 256, c * 256 + 256)
            km = r.kmask[slot, keys, :]
            s = dot_nt(r.kvb[slot, 0, keys, :], r.q[h, cols, :]) + jnp.concatenate([km] * (TQ // 128), axis=1)
            r.sbuf[h % 2, keys, :] = s
            top = jnp.max(s.reshape(32, 8, TQ), axis=0)
            mx = top if mx is None else jnp.maximum(mx, top)
        return jnp.max(mx, axis=0, keepdims=True)

    def soft(h, top):
        qoff = r.qoff[0:1, cols]
        m_old = r.m[h, 0:1, cols]
        m = jnp.maximum(m_old, top + qoff)
        f = jnp.exp2((m_old - m) * SC)
        low = m - qoff
        r.m[h, :, cols] = jnp.broadcast_to(m, (8, TQ))
        r.cross[h, :, cols] = r.cross[h, :, cols] * f
        sq = r.sq[h, :, cols] * (f * f)
        for c in range(2):
            keys = slice(c * 256, c * 256 + 256)
            p = jnp.exp2((r.sbuf[h % 2, keys, :] - low) * SC)
            sq = sq + fold_sum(p * p)
            r.pbuf[h % 2, keys, :] = p.astype(BF16)
        r.sq[h, :, cols] = sq
        return f

    def extend(h):
        xb = (r.bt[...] * r.bdec[h:h + 1, :]).astype(BF16)
        r.xb[slot, h] = xb
        r.state[h] = r.state[h] + dot_nt(jnp.concatenate([r.vt[slot, 0:128, :], xb], axis=0), xb)

    def apply(h, f):
        both = jnp.concatenate([r.vt[slot], r.xb[slot, h]], axis=0)
        r.acc[h, :, cols] = r.acc[h, :, cols] * f + dot(both, r.pbuf[h % 2])

    polls = dict(polls)
    top = score(0)
    kept = None
    for h in range(HG):
        now = top
        if h + 1 < HG:
            top = score(h + 1)
        f = soft(h, now)
        if first:
            extend(h)
        if h > 0:
            apply(h - 1, kept)
        kept = f
        if h in polls:
            polls[h]()
    apply(HG - 1, kept)


def finish_rows(r, w, qt):
    cols = slice(qt * TQ, (qt + 1) * TQ)
    doc_last = r.aux[1, 8:9, BLK - 1:BLK]
    r.from_prev[...] = jnp.where((r.docq[0:1, cols] == doc_last) & (w.s > 0), jnp.ones((8, TQ), F32), 0.0)
    r.ct[...] = jnp.transpose(r.outer_own[cols, :].astype(F32))
    r.ssq[qt] = jnp.zeros((8, TQ), F32)

    def head(i, _):
        for u in range(2):
            h = i * 2 + u
            a = jnp.exp2(r.csum[pl.ds(h, 1), cols]) * r.from_prev[0:1, :]
            y = dot_nt(r.state[h].astype(BF16), r.outer_own[cols, :])
            inv = 1.0 / r.acc[h, 128:129, cols]
            tf = r.acc[h, 0:128, cols] * inv
            sf = r.stud[h, :, cols] + a * y[0:128, :]
            r.acc[h, 0:128, cols] = tf
            r.stud[h, :, cols] = sf
            r.mixsq[h, :, cols] = (r.mixsq[h, :, cols] + (a * a) * fold_sum(y[128:256, :] * r.ct[...])
                                   - (2.0 * inv) * (r.cross[h, :, cols] + a * fold_sum(r.ct[...] * r.acc[h, 144:XR, cols]))
                                   + (inv * inv) * r.sq[h, :, cols])
            r.ssq[qt, 0:1, :] = r.ssq[qt, 0:1, :] + jnp.sum(fold_sum(tf * tf), axis=0, keepdims=True)
            r.ssq[qt, 1:2, :] = r.ssq[qt, 1:2, :] + jnp.sum(fold_sum(sf * sf), axis=0, keepdims=True)
        return 0
    lax.fori_loop(0, HG // 2, head, 0)


def finish_layout(r, qt):
    cols = slice(qt * TQ, (qt + 1) * TQ)

    def head(h, _):
        r.teach[h, cols, :] = jnp.transpose(r.acc[h, 0:128, cols]).astype(BF16)
        r.student[h, cols, :] = jnp.transpose(r.stud[h, :, cols]).astype(BF16)
        r.err[pl.ds(h, 1), cols] = jnp.sum(r.mixsq[h, :, cols], axis=0, keepdims=True)
        return 0
    lax.fori_loop(0, HG, head, 0)


def ssq_copy(r, w, qt, k):
    return remote(r.ssq.at[qt], r.ssq_all.at[qt, w.g], r.ssq_send.at[qt, k], r.ssq_recv.at[qt, w.g],
                  (w.s, ((w.g + k) % 8) * 2 + w.c))


def ssq_from(r, w, qt, k):
    g = (w.g + 8 - k) % 8
    return remote(r.ssq.at[qt], r.ssq_all.at[qt, g], r.ssq_send.at[qt, k], r.ssq_recv.at[qt, g], (w.s, g * 2 + w.c))


def send_ssq(r, w, qt):
    for k in range(1, 8):
        ssq_copy(r, w, qt, k).start()
    r.ssq_all[qt, pl.ds(w.g, 1)] = r.ssq[qt].reshape(1, 8, TQ)


def gap_rows(qt, chip):
    return pl.ds(pl.multiple_of(qt * TQ + chip * 32, 32), 32)


def gap_lanes(g):
    return pl.ds(pl.multiple_of(g * 1024, 1024), 1024)


def gap_copy(r, w, qt, chip):
    to = chip * 2 + qt
    return remote(r.gap.at[gap_rows(qt, chip)], r.out.at[w.c, :, gap_lanes(w.g)],
                  r.out_send.at[to], r.out_recv.at[w.hd], (w.s, to))


def gap_stay(r, w):
    return pltpu.make_async_copy(r.gap.at[gap_rows(w.c, w.g)], r.out.at[w.c, :, gap_lanes(w.g)], r.out_send.at[w.hd])


def send_gap(r, w, qt):
    for k in range(1, 8):
        ssq_from(r, w, qt, k).wait_recv()
    sums = jnp.sum(r.ssq_all[qt], axis=0)
    r.scale[...] = to_columns(lax.rsqrt(sums / (8.0 * HG * 128) + EPS))
    gain = r.gain[pl.ds(pl.multiple_of(w.g * 1024, 1024), 1024)].reshape(1, 1024)

    def one(k, _):
        chip = (w.g + k) % 8
        rows = gap_rows(qt, chip)
        scale = r.scale[pl.ds(pl.multiple_of(chip * 32, 32), 32), :]
        t_scale, s_scale = scale[:, 0:1], scale[:, 1:2]
        for h in range(HG):
            lanes = slice(h * 128, (h + 1) * 128)
            gap = gain[:, lanes] * r.student[h, rows, :].astype(F32) * s_scale - r.teach[h, rows, :].astype(F32) * t_scale
            r.gap[rows, lanes] = gap.astype(BF16)
        stays = (k == 8) & (w.c == qt)

        @pl.when(stays)
        def _():
            gap_stay(r, w).start()

        @pl.when(jnp.logical_not(stays))
        def _():
            gap_copy(r, w, qt, chip).start()
        return 0
    lax.fori_loop(1, 9, one, 0)


def err_copy(r, w, seq):
    return remote(r.err_pair.at[1], r.err_out.at[seq], r.swap_send.at[2], r.swap_recv.at[2], w.sibling)


def send_err(r, w):
    cols = to_columns(r.err[...])
    back = sorted((pos, at) for pos, at in CHUNKS)
    err = jnp.transpose(jnp.concatenate([cols[at:at + 32] for _, at in back], axis=0))
    top, bottom = err[0:4, :], err[4:8, :]
    r.err_pair[0] = jnp.where(w.c == 0, top, bottom)
    r.err_pair[1] = jnp.where(w.c == 0, bottom, top)
    err_copy(r, w, w.c).start()
    near = pltpu.make_async_copy(r.err_pair.at[0], r.err_out.at[w.c], r.load_sem.at[0])
    near.start()
    near.wait()


def end_share(r, w):
    gap_stay(r, w).wait()
    err_copy(r, w, w.c).wait_send()
    err_copy(r, w, 1 - w.c).wait_recv()
    for k in range(1, 8):
        for qt in range(2):
            ssq_copy(r, w, qt, k).wait_send()

    def arrived(k, _):
        sender = (w.hd + k) % 16
        remote(r.gap.at[0:32], r.out.at[sender % 2, :, gap_lanes(sender // 2)],
               r.out_send.at[sender], r.out_recv.at[sender], (w.s, sender)).wait_recv()
        gap_copy(r, w, sender % 2, sender // 2).wait_send()
        return 0
    lax.fori_loop(1, 16, arrived, 0)


ARGS = ("query", "key", "value", "inner", "outer", "decay", "docs", "gain")
OUTS = ("out", "err_out")
DMA = pltpu.SemaphoreType.DMA
SCRATCH = dict(
    qraw=pltpu.VMEM((2, 2048, 128), BF16), decay_raw=pltpu.VMEM((2, 4, BLK), F32),
    raw=pltpu.VMEM((4, 4096, 128), BF16), wide=pltpu.VMEM((4096, 128), F32),
    q=pltpu.VMEM((HG, BLK, 128), BF16), kvb=pltpu.VMEM((SLOTS, 3, BLK, 128), BF16),
    aux=pltpu.VMEM((SLOTS, 16, BLK), F32), outer_own=pltpu.VMEM((BLK, 128), BF16),
    csum=pltpu.VMEM((8, BLK), F32), csum_col=pltpu.VMEM((BLK, 128), F32), docq=pltpu.VMEM((8, BLK), F32),
    cb=pltpu.VMEM((BLK, BLK), F32), hide=pltpu.VMEM((BLK, BLK), F32),
    m=pltpu.VMEM((HG, 8, BLK), F32), sq=pltpu.VMEM((HG, 8, BLK), F32),
    cross=pltpu.VMEM((HG, 8, BLK), F32), mixsq=pltpu.VMEM((HG, 8, BLK), F32),
    acc=pltpu.VMEM((HG, XR, BLK), F32), stud=pltpu.VMEM((HG, 128, BLK), F32),
    state=pltpu.VMEM((HG, 256, 128), F32), bdec=pltpu.VMEM((8, BLK), F32),
    kmask=pltpu.VMEM((SLOTS, BLK, 128), F32), qoff=pltpu.VMEM((8, BLK), F32),
    vt=pltpu.VMEM((SLOTS, 144, BLK), BF16), xb=pltpu.VMEM((SLOTS, HG, 128, BLK), BF16), bt=pltpu.VMEM((128, BLK), F32),
    sbuf=pltpu.VMEM((2, BLK, TQ), F32), pbuf=pltpu.VMEM((2, BLK, TQ), BF16), mbuf=pltpu.VMEM((2, BLK, TQ), BF16),
    ct=pltpu.VMEM((128, TQ), F32), from_prev=pltpu.VMEM((8, TQ), F32), scale=pltpu.VMEM((TQ, 128), F32),
    teach=pltpu.VMEM((HG, BLK, 128), BF16), student=pltpu.VMEM((HG, BLK, 128), BF16),
    err=pltpu.VMEM((8, BLK), F32), err_pair=pltpu.VMEM((2, 4, BLK), F32),
    ssq=pltpu.VMEM((2, 8, TQ), F32), ssq_all=pltpu.VMEM((2, 8, 8, TQ), F32), gap=pltpu.VMEM((BLK, HG * 128), BF16),
    load_sem=DMA((6,)), swap_send=DMA((3,)), swap_recv=DMA((3,)),
    up_send=DMA((2, 4)), up_recv=DMA((2, 4)), side_send=DMA((2, 4)), side_recv=DMA((2, 4)),
    ssq_send=DMA((2, 8)), ssq_recv=DMA((2, 8)), out_send=DMA((16,)), out_recv=DMA((16,)),
)


def kernel(*refs):
    r = Refs()
    for name, ref in zip(ARGS + OUTS + tuple(SCRATCH), refs):
        setattr(r, name, ref)
    w = Place()
    load_own(r, w)
    own_prepare(r)
    own_half(r, 0, {2: lambda: take_up(r, w, 0, (0,)), 7: lambda: take_up(r, w, 0, (1,))})
    own_half(r, 1, {5: lambda: take_up(r, w, 0, (2, 3))})

    @pl.when(w.s == 0)
    def _():
        r.aux[1] = jnp.zeros((16, BLK), F32)

    @pl.when(gets_side(w, 0))
    def _():
        side_copy(r, w, 0, 3).wait_recv()

    @pl.when(w.s >= 2)
    def _():
        prepare(r, 2)
        slot_half(r, 2, 0, True, {3: lambda: take_up(r, w, 1, (0,))})
        slot_half(r, 2, 1, False, {5: lambda: take_up(r, w, 1, (1,))})

    @pl.when(w.s >= 1)
    def _():
        take_side(r, w, 0, (0, 1, 2))
        prepare(r, 1)
        slot_half(r, 1, 0, True, {2: lambda: take_up(r, w, 1, (2, 3))})

    @pl.when(w.s >= 3)
    def _():
        take_side(r, w, 1, (3,))

    @pl.when(w.s >= 4)
    def _():
        prepare(r, 4)
        slot_half(r, 4, 0, True)

    @pl.when(w.s >= 3)
    def _():
        take_side(r, w, 1, (0, 1, 2))
        prepare(r, 3)
        slot_half(r, 3, 0, True)
    finish_rows(r, w, 0)
    send_ssq(r, w, 0)
    finish_layout(r, 0)

    @pl.when(w.s >= 1)
    def _():
        slot_half(r, 1, 1, False)
    send_gap(r, w, 0)

    @pl.when(w.s >= 4)
    def _():
        slot_half(r, 4, 1, False)

    @pl.when(w.s >= 3)
    def _():
        slot_half(r, 3, 1, False)
    finish_rows(r, w, 1)
    send_ssq(r, w, 1)
    finish_layout(r, 1)
    send_err(r, w)
    send_gap(r, w, 1)
    end_share(r, w)
    end_sends(r, w)


def settle(out, err, out_to, err_to):
    out_to[...] = out[...]
    err_to[...] = err[...]


def on_device(query_rows, key_rows, value_rows, state_in, state_out, log_decay, doc_ids, norm_gain):
    flat = [x.reshape(2, -1, 128) for x in (query_rows, key_rows, value_rows, state_in, state_out)]
    shapes = (jax.ShapeDtypeStruct((2, 32, 8192), BF16), jax.ShapeDtypeStruct((2, 4, BLK), F32))
    anywhere = pl.BlockSpec(memory_space=pl.ANY)
    landed = pl.pallas_call(
        kernel,
        out_shape=shapes,
        in_specs=[pl.BlockSpec(memory_space=pl.ANY)] * 6 + [pl.BlockSpec(memory_space=pltpu.VMEM)] * 2,
        out_specs=(pl.BlockSpec(memory_space=pl.ANY), pl.BlockSpec(memory_space=pl.ANY)),
        scratch_shapes=list(SCRATCH.values()),
        compiler_params=pltpu.CompilerParams(collective_id=0, has_side_effects=True, vmem_limit_bytes=56 * 2**20),
        cost_estimate=pl.CostEstimate(flops=10**10, bytes_accessed=10**7, transcendentals=0),
    )(*flat, log_decay, doc_ids, norm_gain)
    half = pl.BlockSpec((1, 32, 8192), lambda i: (i, 0, 0))
    quarter = pl.BlockSpec((1, 4, BLK), lambda i: (i, 0, 0))
    return pl.pallas_call(
        settle,
        out_shape=shapes,
        grid=(2,),
        in_specs=[half, quarter],
        out_specs=(half, quarter),
    )(*landed)


def solution(mesh):
    placed = (
        P(None, "seq", "head", None),
        P(None, "seq", None, None),
        P(None, "seq", None, None),
        P(None, "seq", None, None),
        P(None, "seq", None, None),
        P(None, "head", "seq"),
        P(None, "seq"),
        P(),
    )
    return jax.shard_map(
        on_device,
        mesh=mesh,
        in_specs=placed,
        out_specs=(P(None, ("seq", "head"), None), P(None, "head", "seq")),
        check_vma=False,
    )
```

```python
import math

import jax
import jax.numpy as jnp
from jax import lax
from jax.experimental import pallas as pl
from jax.experimental.pallas import tpu as pltpu
from jax.sharding import PartitionSpec as P

F32, BF16 = jnp.float32, jnp.bfloat16
BLK, HG, SLOTS, TQ = 512, 8, 5, 256
XR = 272
LOG2E = 1.4426950408889634
SC = LOG2E / math.sqrt(128.0)
BIG = 1e30
EPS = 1e-05
NT = (((1,), (1,)), ((), ()))
MESH = pl.DeviceIdType.MESH


def dot_nt(a, b):
    return lax.dot_general(a, b, NT, preferred_element_type=F32)


def dot(a, b):
    return jnp.dot(a, b, preferred_element_type=F32)


def fold_sum(x):
    return jnp.sum(x.reshape(x.shape[0] // 8, 8, x.shape[1]), axis=0)


def fold_max(x):
    return jnp.max(jnp.max(x.reshape(x.shape[0] // 8, 8, x.shape[1]), axis=0), axis=0, keepdims=True)


def prefix_sums(x):
    lane = lax.broadcasted_iota(jnp.int32, x.shape, 1)
    step = 1
    while step < x.shape[1]:
        x = x + jnp.where(lane >= step, pltpu.roll(x, step, 1), 0.0)
        step *= 2
    return x


def to_columns(rows):
    wide = jnp.concatenate([rows, jnp.zeros((128 - rows.shape[0], rows.shape[1]), F32)], axis=0)
    return jnp.transpose(wide)


def t16(x):
    return jnp.transpose(x.astype(F32)).astype(BF16)


class Refs:
    pass


class Place:
    def __init__(self):
        self.s, self.hd = lax.axis_index("seq"), lax.axis_index("head")
        self.z, self.col = self.s // 2, self.s % 2
        self.g, self.c = self.hd // 2, self.hd % 2
        self.sibling = (self.s, self.g * 2 + 1 - self.c)
        self.beside = (self.z * 2 + 1 - self.col, self.hd)
        self.above = (self.s + 2, self.hd)
        self.below = (self.s - 2, self.hd)


def remote(src, dst, send, recv, device):
    return pltpu.make_async_remote_copy(
        src_ref=src, dst_ref=dst, send_sem=send, recv_sem=recv, device_id=device, device_id_type=MESH)


def greet(w):
    barrier = pltpu.get_barrier_semaphore()

    def tell(device):
        pl.semaphore_signal(barrier, inc=1, device_id=device, device_id_type=MESH)

    def others(k, _):
        tell((w.s, (w.hd + k) % 16))
        return 0
    lax.fori_loop(1, 16, others, 0)
    tell(w.beside)

    @pl.when(w.z < 3)
    def _():
        tell(w.above)

    @pl.when(w.z > 0)
    def _():
        tell(w.below)
    pl.semaphore_wait(barrier, 16 + (w.z + 2) // 3 + (5 - w.z) // 3 - 0)


def swap_copies(r, w):
    return (remote(r.query.at[1 - w.c], r.qraw.at[1], r.swap_send.at[0], r.swap_recv.at[0], w.sibling),
            remote(r.decay.at[1 - w.c], r.decay_raw.at[1], r.swap_send.at[1], r.swap_recv.at[1], w.sibling))


def spread(p):
    return (p % 256) // 32 * 64 + p // 256 * 32 + p % 32


CHUNKS = [(spread(32 * i), 32 * i) for i in range(16)]


def part(r, slot, j):
    return r.aux.at[slot] if j == 3 else r.kvb.at[slot, j]


def up_copy(r, w, step, j):
    return remote(part(r, 2 * step, j), part(r, 2 * step + 2, j), r.up_send.at[step, j], r.up_recv.at[step, j], w.above)


def side_copy(r, w, step, j):
    return remote(part(r, 2 * step + 2 * w.col, j), part(r, 2 * step + 1, j), r.side_send.at[step, j], r.side_recv.at[step, j], w.beside)


def sends_up(w, step):
    return (w.z < 3) if step == 0 else ((w.z >= 1) & (w.z < 3))


def sends_side(w, step):
    return w.z >= step + w.col


def gets_up(w, step):
    return w.z >= step + 1


def gets_side(w, step):
    return w.z >= step + 1 - w.col


def load_own(r, w):
    loads = [pltpu.make_async_copy(ref.at[w.c], r.raw.at[i], r.load_sem.at[i])
             for i, ref in enumerate((r.key, r.value, r.inner, r.outer))]
    qload = pltpu.make_async_copy(r.query.at[w.c], r.qraw.at[0], r.load_sem.at[4])
    aload = pltpu.make_async_copy(r.decay.at[w.c], r.decay_raw.at[0], r.load_sem.at[5])
    aload.start()
    for x in loads:
        x.start()
    qload.start()
    greet(w)
    swaps = swap_copies(r, w)
    swaps[1].start()
    swaps[0].start()

    def send_part(j):
        @pl.when(sends_up(w, 0))
        def _():
            up_copy(r, w, 0, j).start()

        @pl.when((w.col == 0) & sends_side(w, 0))
        def _():
            side_copy(r, w, 0, j).start()

    def send_small():
        aload.wait()
        swaps[1].wait_recv()
        mine, theirs = r.decay_raw[0], r.decay_raw[1]
        first = jnp.where(w.c == 0, mine, theirs)
        second = jnp.where(w.c == 0, theirs, mine)
        r.aux[0, 0:8, :] = jnp.concatenate([first, second], axis=0)
        docs = jnp.where(w.c == 0, r.docs[0:1, :], r.docs[1:2, :]).astype(F32)
        r.aux[0, 8:16, :] = jnp.broadcast_to(docs, (8, BLK))
        send_part(3)

    for i in range(4):
        loads[i].wait()
        r.wide[...] = r.raw[i].astype(F32)
        if i < 3:
            r.kvb[0, i] = r.wide[pl.ds(w.g, BLK, stride=8), :].astype(BF16)
            send_part(i)
            if i == 0:
                send_small()
        else:
            for pos, to in CHUNKS:
                r.outer_own[to:to + 32, :] = r.wide[pl.ds(w.g + 8 * pos, 32, stride=8), :].astype(BF16)
    qload.wait()
    swaps[0].wait_recv()
    for i in range(2):
        r.wide[0:2048, :] = r.qraw[i].astype(F32)
        base = 4 * w.c if i == 0 else 4 - 4 * w.c
        for j in range(4):
            for pos, to in CHUNKS:
                r.q[base + j, to:to + 32, :] = r.wide[pl.ds(j + 4 * pos, 32, stride=4), :].astype(BF16)
    for x in swaps:
        x.wait_send()


def take_up(r, w, step, parts):
    @pl.when(gets_up(w, step))
    def _():
        for j in parts:
            up_copy(r, w, step, j).wait_recv()
            if step == 0:
                @pl.when(w.col == 1)
                def _():
                    side_copy(r, w, 0, j).start()

                @pl.when(sends_up(w, 1))
                def _():
                    up_copy(r, w, 1, j).start()

                @pl.when(w.col == 0)
                def _():
                    side_copy(r, w, 1, j).start()
            else:
                @pl.when(w.col == 1)
                def _():
                    side_copy(r, w, 1, j).start()


def take_side(r, w, step, parts):
    for j in parts:
        side_copy(r, w, step, j).wait_recv()


def end_sends(r, w):
    for step in range(2):
        @pl.when(sends_up(w, step))
        def _():
            for j in range(4):
                up_copy(r, w, step, j).wait_send()

        @pl.when(sends_side(w, step))
        def _():
            for j in range(4):
                side_copy(r, w, step, j).wait_send()


def own_prepare(r):
    own = prefix_sums(r.aux[0, 0:8, :]) * LOG2E
    cols = to_columns(jnp.concatenate([own, r.aux[0, 8:16, :]], axis=0))
    r.csum_col[...] = cols
    rows = jnp.transpose(jnp.concatenate([cols[pos:pos + 32] for pos, _ in CHUNKS], axis=0))
    r.csum[...] = rows[0:8]
    r.docq[...] = rows[8:16]
    doc_c = cols[:, 8:9]
    cb = dot_nt(r.kvb[0, 2], r.outer_own[...])
    kj = lax.broadcasted_iota(jnp.int32, (BLK, BLK), 0)
    qi = spread(lax.broadcasted_iota(jnp.int32, (BLK, BLK), 1))
    seen = (qi >= kj) & (doc_c == r.docq[0:1, :])
    r.cb[...] = jnp.where(seen, cb, 0.0)
    r.hide[...] = jnp.where(seen, 0.0, -BIG)
    for slot in range(SLOTS):
        r.vt[slot, 128:144, :] = jnp.ones((16, BLK), BF16)
    r.vt[0, 0:128, :] = t16(r.kvb[0, 1])


def late(x):
    return jnp.concatenate([jnp.zeros_like(x), x], axis=1)


def own_half(r, qt, polls=()):
    base = qt * TQ
    parts = ((slice(0, 256), slice(0, 256)), (slice(256, 512), slice(128, 256)))
    cols = slice(base, base + TQ)
    polls = dict(polls)
    for at in range(2):
        r.pbuf[at, 256:512, 0:128] = jnp.zeros((256, 128), BF16)
        r.mbuf[at, 256:512, 0:128] = jnp.zeros((256, 128), BF16)

    def score(h):
        tops = []
        for keys, part_cols in parts:
            here = slice(base + part_cols.start, base + part_cols.stop)
            s = dot_nt(r.kvb[0, 0, keys, :], r.q[h, here, :]) + r.hide[keys, here]
            r.sbuf[h % 2, keys, part_cols] = s
            tops.append(jnp.max(s.reshape(32, 8, s.shape[1]), axis=0))
        both = jnp.concatenate([tops[0][:, 0:128], jnp.maximum(tops[0][:, 128:256], tops[1])], axis=1)
        return jnp.max(both, axis=0, keepdims=True)

    def soft(h, m):
        r.m[h, :, cols] = jnp.broadcast_to(m, (8, TQ))
        sums = []
        for keys, part_cols in parts:
            here = slice(base + part_cols.start, base + part_cols.stop)
            p = jnp.exp2((r.sbuf[h % 2, keys, part_cols] - m[:, part_cols]) * SC)
            fall = jnp.minimum(r.csum[h:h + 1, here] - r.csum_col[keys, h:h + 1], 0.0)
            mix = jnp.exp2(fall) * r.cb[keys, here]
            sums.append((fold_sum(p * p), fold_sum(p * mix), fold_sum(mix * mix)))
            r.pbuf[h % 2, keys, part_cols] = p.astype(BF16)
            r.mbuf[h % 2, keys, part_cols] = mix.astype(BF16)
        r.sq[h, :, cols], r.cross[h, :, cols], r.mixsq[h, :, cols] = (x + late(y) for x, y in zip(*sums))

    def apply(h):
        r.acc[h, 0:144, cols] = dot(r.vt[0], r.pbuf[h % 2])
        r.acc[h, 144:XR, cols] = jnp.zeros((128, TQ), F32)
        r.stud[h, :, cols] = dot(r.vt[0, 0:128, :], r.mbuf[h % 2])
        if qt == 0:
            r.state[h] = jnp.zeros((256, 128), F32)

    top = score(0)
    for h in range(HG):
        now = top
        if h + 1 < HG:
            top = score(h + 1)
        soft(h, now)
        if h > 0:
            apply(h - 1)
        if h in polls:
            polls[h]()
    apply(HG - 1)


def prepare(r, slot):
    sums = prefix_sums(r.aux[slot, 0:8, :])
    whole = sums[:, BLK - 1:BLK]
    doc_last = r.aux[1, 8:9, BLK - 1:BLK]
    tail = jnp.zeros((8, 1), F32)
    for t in range(1, slot):
        tail = tail + jnp.sum(r.aux[t, 0:8, :], axis=1, keepdims=True)
    weight = jnp.exp(whole - sums + tail)
    r.bdec[...] = jnp.where(r.aux[slot, 8:9, :] == doc_last, weight, 0.0)
    doc_c = to_columns(r.aux[slot, 8:16, :])[:, 0:1]
    r.kmask[slot] = jnp.broadcast_to(jnp.where(doc_c == doc_last, 0.0, -BIG), (BLK, 128))
    r.qoff[...] = jnp.broadcast_to(jnp.where(r.docq[0:1, :] == doc_last, 0.0, -BIG), (8, BLK))
    r.vt[slot, 0:128, :] = t16(r.kvb[slot, 1])
    r.bt[...] = jnp.transpose(r.kvb[slot, 2].astype(F32))


def slot_half(r, slot, qt, first, polls=()):
    base = qt * TQ
    cols = slice(base, base + TQ)
    far = slot == SLOTS - 1
    parts = ((slice(0, 256), slice(0, 128 if far else 256)), (slice(256, 512), slice(0, 256)))
    if far:
        for at in range(2):
            r.pbuf[at, 0:256, 128:256] = jnp.zeros((256, 128), BF16)

    def score(h):
        tops = []
        for keys, part_cols in parts:
            km = r.kmask[slot, keys, :]
            s = dot_nt(r.kvb[slot, 0, keys, :], r.q[h, base:base + part_cols.stop, :])
            s = s + jnp.concatenate([km] * (part_cols.stop // 128), axis=1)
            r.sbuf[h % 2, keys, part_cols] = s
            tops.append(jnp.max(s.reshape(32, 8, part_cols.stop), axis=0))
        if far:
            mx = jnp.concatenate([jnp.maximum(tops[0], tops[1][:, 0:128]), tops[1][:, 128:256]], axis=1)
        else:
            mx = jnp.maximum(*tops)
        return jnp.max(mx, axis=0, keepdims=True)

    def soft(h, top):
        qoff = r.qoff[0:1, cols]
        m_old = r.m[h, 0:1, cols]
        m = jnp.maximum(m_old, top + qoff)
        f = jnp.exp2((m_old - m) * SC)
        low = m - qoff
        r.m[h, :, cols] = jnp.broadcast_to(m, (8, TQ))
        r.cross[h, :, cols] = r.cross[h, :, cols] * f
        sq = r.sq[h, :, cols] * (f * f)
        for keys, part_cols in parts:
            p = jnp.exp2((r.sbuf[h % 2, keys, part_cols] - low[:, part_cols]) * SC)
            more = fold_sum(p * p)
            if part_cols.stop < TQ:
                more = jnp.concatenate([more, jnp.zeros_like(more)], axis=1)
            sq = sq + more
            r.pbuf[h % 2, keys, part_cols] = p.astype(BF16)
        r.sq[h, :, cols] = sq
        return f

    def extend(h):
        xb = (r.bt[...] * r.bdec[h:h + 1, :]).astype(BF16)
        r.xb[slot, h] = xb
        r.state[h] = r.state[h] + dot_nt(jnp.concatenate([r.vt[slot, 0:128, :], xb], axis=0), xb)

    def apply(h, f):
        both = jnp.concatenate([r.vt[slot], r.xb[slot, h]], axis=0)
        r.acc[h, :, cols] = r.acc[h, :, cols] * f + dot(both, r.pbuf[h % 2])

    polls = dict(polls)
    top = score(0)
    kept = None
    for h in range(HG):
        now = top
        if h + 1 < HG:
            top = score(h + 1)
        f = soft(h, now)
        if first:
            extend(h)
        if h > 0:
            apply(h - 1, kept)
        kept = f
        if h in polls:
            polls[h]()
    apply(HG - 1, kept)


def finish_rows(r, w, qt):
    cols = slice(qt * TQ, (qt + 1) * TQ)
    doc_last = r.aux[1, 8:9, BLK - 1:BLK]
    r.from_prev[...] = jnp.where((r.docq[0:1, cols] == doc_last) & (w.s > 0), jnp.ones((8, TQ), F32), 0.0)
    r.ct[...] = jnp.transpose(r.outer_own[cols, :].astype(F32))
    r.ssq[qt] = jnp.zeros((8, TQ), F32)

    def head(i, _):
        for u in range(2):
            h = i * 2 + u
            a = jnp.exp2(r.csum[pl.ds(h, 1), cols]) * r.from_prev[0:1, :]
            y = dot_nt(r.state[h].astype(BF16), r.outer_own[cols, :])
            inv = 1.0 / r.acc[h, 128:129, cols]
            tf = r.acc[h, 0:128, cols] * inv
            sf = r.stud[h, :, cols] + a * y[0:128, :]
            r.acc[h, 0:128, cols] = tf
            r.stud[h, :, cols] = sf
            r.mixsq[h, :, cols] = (r.mixsq[h, :, cols] + (a * a) * fold_sum(y[128:256, :] * r.ct[...])
                                   - (2.0 * inv) * (r.cross[h, :, cols] + a * fold_sum(r.ct[...] * r.acc[h, 144:XR, cols]))
                                   + (inv * inv) * r.sq[h, :, cols])
            r.ssq[qt, 0:1, :] = r.ssq[qt, 0:1, :] + jnp.sum(fold_sum(tf * tf), axis=0, keepdims=True)
            r.ssq[qt, 1:2, :] = r.ssq[qt, 1:2, :] + jnp.sum(fold_sum(sf * sf), axis=0, keepdims=True)
        return 0
    lax.fori_loop(0, HG // 2, head, 0)


def finish_layout(r, qt):
    cols = slice(qt * TQ, (qt + 1) * TQ)

    def head(h, _):
        r.teach[h, cols, :] = jnp.transpose(r.acc[h, 0:128, cols]).astype(BF16)
        r.student[h, cols, :] = jnp.transpose(r.stud[h, :, cols]).astype(BF16)
        r.err[pl.ds(h, 1), cols] = jnp.sum(r.mixsq[h, :, cols], axis=0, keepdims=True)
        return 0
    lax.fori_loop(0, HG, head, 0)


def ssq_copy(r, w, qt, k):
    return remote(r.ssq.at[qt], r.ssq_all.at[qt, w.g], r.ssq_send.at[qt, k], r.ssq_recv.at[qt, w.g],
                  (w.s, ((w.g + k) % 8) * 2 + w.c))


def ssq_from(r, w, qt, k):
    g = (w.g + 8 - k) % 8
    return remote(r.ssq.at[qt], r.ssq_all.at[qt, g], r.ssq_send.at[qt, k], r.ssq_recv.at[qt, g], (w.s, g * 2 + w.c))


def send_ssq(r, w, qt):
    for k in range(1, 8):
        ssq_copy(r, w, qt, k).start()
    r.ssq_all[qt, pl.ds(w.g, 1)] = r.ssq[qt].reshape(1, 8, TQ)


def gap_rows(qt, chip):
    return pl.ds(pl.multiple_of(qt * TQ + chip * 32, 32), 32)


def gap_lanes(g):
    return pl.ds(pl.multiple_of(g * 1024, 1024), 1024)


def gap_copy(r, w, qt, chip):
    to = chip * 2 + qt
    return remote(r.gap.at[gap_rows(qt, chip)], r.out.at[w.c, :, gap_lanes(w.g)],
                  r.out_send.at[to], r.out_recv.at[w.hd], (w.s, to))


def gap_stay(r, w):
    return pltpu.make_async_copy(r.gap.at[gap_rows(w.c, w.g)], r.out.at[w.c, :, gap_lanes(w.g)], r.out_send.at[w.hd])


def send_gap(r, w, qt):
    for k in range(1, 8):
        ssq_from(r, w, qt, k).wait_recv()
    sums = jnp.sum(r.ssq_all[qt], axis=0)
    r.scale[...] = to_columns(lax.rsqrt(sums / (8.0 * HG * 128) + EPS))
    gain = r.gain[pl.ds(pl.multiple_of(w.g * 1024, 1024), 1024)].reshape(1, 1024)

    def one(k, _):
        chip = (w.g + k) % 8
        rows = gap_rows(qt, chip)
        scale = r.scale[pl.ds(pl.multiple_of(chip * 32, 32), 32), :]
        t_scale, s_scale = scale[:, 0:1], scale[:, 1:2]
        for h in range(HG):
            lanes = slice(h * 128, (h + 1) * 128)
            gap = gain[:, lanes] * r.student[h, rows, :].astype(F32) * s_scale - r.teach[h, rows, :].astype(F32) * t_scale
            r.gap[rows, lanes] = gap.astype(BF16)
        stays = (k == 8) & (w.c == qt)

        @pl.when(stays)
        def _():
            gap_stay(r, w).start()

        @pl.when(jnp.logical_not(stays))
        def _():
            gap_copy(r, w, qt, chip).start()
        return 0
    lax.fori_loop(1, 9, one, 0)


def err_copy(r, w, seq):
    return remote(r.err_pair.at[1], r.err_out.at[seq], r.swap_send.at[2], r.swap_recv.at[2], w.sibling)


def send_err(r, w):
    cols = to_columns(r.err[...])
    back = sorted((pos, at) for pos, at in CHUNKS)
    err = jnp.transpose(jnp.concatenate([cols[at:at + 32] for _, at in back], axis=0))
    top, bottom = err[0:4, :], err[4:8, :]
    r.err_pair[0] = jnp.where(w.c == 0, top, bottom)
    r.err_pair[1] = jnp.where(w.c == 0, bottom, top)
    err_copy(r, w, w.c).start()
    near = pltpu.make_async_copy(r.err_pair.at[0], r.err_out.at[w.c], r.load_sem.at[0])
    near.start()
    near.wait()


def end_share(r, w):
    gap_stay(r, w).wait()
    err_copy(r, w, w.c).wait_send()
    err_copy(r, w, 1 - w.c).wait_recv()
    for k in range(1, 8):
        for qt in range(2):
            ssq_copy(r, w, qt, k).wait_send()

    def arrived(k, _):
        sender = (w.hd + k) % 16
        remote(r.gap.at[0:32], r.out.at[sender % 2, :, gap_lanes(sender // 2)],
               r.out_send.at[sender], r.out_recv.at[sender], (w.s, sender)).wait_recv()
        gap_copy(r, w, sender % 2, sender // 2).wait_send()
        return 0
    lax.fori_loop(1, 16, arrived, 0)


ARGS = ("query", "key", "value", "inner", "outer", "decay", "docs", "gain")
OUTS = ("out", "err_out")
DMA = pltpu.SemaphoreType.DMA
SCRATCH = dict(
    qraw=pltpu.VMEM((2, 2048, 128), BF16), decay_raw=pltpu.VMEM((2, 4, BLK), F32),
    raw=pltpu.VMEM((4, 4096, 128), BF16), wide=pltpu.VMEM((4096, 128), F32),
    q=pltpu.VMEM((HG, BLK, 128), BF16), kvb=pltpu.VMEM((SLOTS, 3, BLK, 128), BF16),
    aux=pltpu.VMEM((SLOTS, 16, BLK), F32), outer_own=pltpu.VMEM((BLK, 128), BF16),
    csum=pltpu.VMEM((8, BLK), F32), csum_col=pltpu.VMEM((BLK, 128), F32), docq=pltpu.VMEM((8, BLK), F32),
    cb=pltpu.VMEM((BLK, BLK), F32), hide=pltpu.VMEM((BLK, BLK), F32),
    m=pltpu.VMEM((HG, 8, BLK), F32), sq=pltpu.VMEM((HG, 8, BLK), F32),
    cross=pltpu.VMEM((HG, 8, BLK), F32), mixsq=pltpu.VMEM((HG, 8, BLK), F32),
    acc=pltpu.VMEM((HG, XR, BLK), F32), stud=pltpu.VMEM((HG, 128, BLK), F32),
    state=pltpu.VMEM((HG, 256, 128), F32), bdec=pltpu.VMEM((8, BLK), F32),
    kmask=pltpu.VMEM((SLOTS, BLK, 128), F32), qoff=pltpu.VMEM((8, BLK), F32),
    vt=pltpu.VMEM((SLOTS, 144, BLK), BF16), xb=pltpu.VMEM((SLOTS, HG, 128, BLK), BF16), bt=pltpu.VMEM((128, BLK), F32),
    sbuf=pltpu.VMEM((2, BLK, TQ), F32), pbuf=pltpu.VMEM((2, BLK, TQ), BF16), mbuf=pltpu.VMEM((2, BLK, TQ), BF16),
    ct=pltpu.VMEM((128, TQ), F32), from_prev=pltpu.VMEM((8, TQ), F32), scale=pltpu.VMEM((TQ, 128), F32),
    teach=pltpu.VMEM((HG, BLK, 128), BF16), student=pltpu.VMEM((HG, BLK, 128), BF16),
    err=pltpu.VMEM((8, BLK), F32), err_pair=pltpu.VMEM((2, 4, BLK), F32),
    ssq=pltpu.VMEM((2, 8, TQ), F32), ssq_all=pltpu.VMEM((2, 8, 8, TQ), F32), gap=pltpu.VMEM((BLK, HG * 128), BF16),
    load_sem=DMA((6,)), swap_send=DMA((3,)), swap_recv=DMA((3,)),
    up_send=DMA((2, 4)), up_recv=DMA((2, 4)), side_send=DMA((2, 4)), side_recv=DMA((2, 4)),
    ssq_send=DMA((2, 8)), ssq_recv=DMA((2, 8)), out_send=DMA((16,)), out_recv=DMA((16,)),
)


def kernel(*refs):
    r = Refs()
    for name, ref in zip(ARGS + OUTS + tuple(SCRATCH), refs):
        setattr(r, name, ref)
    w = Place()
    load_own(r, w)
    own_prepare(r)
    own_half(r, 0, {4: lambda: take_up(r, w, 0, (0, 3))})
    own_half(r, 1, {0: lambda: take_up(r, w, 0, (1,)), 7: lambda: take_up(r, w, 0, (2,))})

    @pl.when(w.s == 0)
    def _():
        r.aux[1] = jnp.zeros((16, BLK), F32)

    @pl.when(gets_side(w, 0))
    def _():
        side_copy(r, w, 0, 3).wait_recv()

    @pl.when(w.s >= 2)
    def _():
        prepare(r, 2)
        slot_half(r, 2, 0, True, {7: lambda: take_up(r, w, 1, (0, 3))})
        slot_half(r, 2, 1, False, {7: lambda: take_up(r, w, 1, (1,))})

    @pl.when(w.s >= 1)
    def _():
        take_side(r, w, 0, (0, 1, 2))
        prepare(r, 1)
        slot_half(r, 1, 0, True)
        slot_half(r, 1, 1, False, {0: lambda: take_up(r, w, 1, (2,))})

    @pl.when(w.s >= 3)
    def _():
        take_side(r, w, 1, (3,))

    @pl.when(w.s >= 4)
    def _():
        prepare(r, 4)
        slot_half(r, 4, 0, True)

    @pl.when(w.s >= 3)
    def _():
        take_side(r, w, 1, (0, 1, 2))
        prepare(r, 3)
        slot_half(r, 3, 0, True)
    finish_rows(r, w, 0)
    send_ssq(r, w, 0)
    finish_layout(r, 0)

    @pl.when(w.s >= 4)
    def _():
        slot_half(r, 4, 1, False, {4: lambda: send_gap(r, w, 0)})

    @pl.when(w.s < 4)
    def _():
        send_gap(r, w, 0)

    @pl.when(w.s >= 3)
    def _():
        slot_half(r, 3, 1, False)
    finish_rows(r, w, 1)
    send_ssq(r, w, 1)
    finish_layout(r, 1)
    send_err(r, w)
    send_gap(r, w, 1)
    end_share(r, w)
    end_sends(r, w)


def on_device(query_rows, key_rows, value_rows, state_in, state_out, log_decay, doc_ids, norm_gain):
    flat = [x.reshape(2, -1, 128) for x in (query_rows, key_rows, value_rows, state_in, state_out)]
    shapes = (jax.ShapeDtypeStruct((2, 32, 8192), BF16), jax.ShapeDtypeStruct((2, 4, BLK), F32))
    landed = pl.pallas_call(
        kernel,
        out_shape=(pltpu.VMEM(shapes[0].shape, BF16), shapes[1]),
        in_specs=[pl.BlockSpec(memory_space=pl.ANY)] * 6 + [pl.BlockSpec(memory_space=pltpu.VMEM)] * 2,
        out_specs=(pl.BlockSpec(memory_space=pltpu.VMEM), pl.BlockSpec(memory_space=pl.ANY)),
        scratch_shapes=list(SCRATCH.values()),
        compiler_params=pltpu.CompilerParams(collective_id=0, has_side_effects=True, vmem_limit_bytes=56 * 2**20),
        cost_estimate=pl.CostEstimate(flops=10**10, bytes_accessed=10**7, transcendentals=0),
    )(*flat, log_decay, doc_ids, norm_gain)
    return landed


def solution(mesh):
    placed = (
        P(None, "seq", "head", None),
        P(None, "seq", None, None),
        P(None, "seq", None, None),
        P(None, "seq", None, None),
        P(None, "seq", None, None),
        P(None, "head", "seq"),
        P(None, "seq"),
        P(),
    )
    return jax.shard_map(
        on_device,
        mesh=mesh,
        in_specs=placed,
        out_specs=(P(None, ("seq", "head"), None), P(None, "head", "seq")),
        check_vma=False,
    )
```

```python
import math

import jax
import jax.numpy as jnp
from jax import lax
from jax.experimental import pallas as pl
from jax.experimental.pallas import tpu as pltpu
from jax.sharding import PartitionSpec as P

F32, BF16 = jnp.float32, jnp.bfloat16
BLK, HG, SLOTS, TQ = 512, 8, 5, 256
XR = 272
LOG2E = 1.4426950408889634
SC = LOG2E / math.sqrt(128.0)
BIG = 1e30
EPS = 1e-05
NT = (((1,), (1,)), ((), ()))
MESH = pl.DeviceIdType.MESH


def dot_nt(a, b):
    return lax.dot_general(a, b, NT, preferred_element_type=F32)


def dot(a, b):
    return jnp.dot(a, b, preferred_element_type=F32)


def fold_sum(x):
    return jnp.sum(x.reshape(x.shape[0] // 8, 8, x.shape[1]), axis=0)


def fold_max(x):
    return jnp.max(jnp.max(x.reshape(x.shape[0] // 8, 8, x.shape[1]), axis=0), axis=0, keepdims=True)


def prefix_sums(x):
    lane = lax.broadcasted_iota(jnp.int32, x.shape, 1)
    step = 1
    while step < x.shape[1]:
        x = x + jnp.where(lane >= step, pltpu.roll(x, step, 1), 0.0)
        step *= 2
    return x


def to_columns(rows):
    wide = jnp.concatenate([rows, jnp.zeros((128 - rows.shape[0], rows.shape[1]), F32)], axis=0)
    return jnp.transpose(wide)


def t16(x):
    return jnp.transpose(x)


class Refs:
    pass


class Place:
    def __init__(self):
        self.s, self.hd = lax.axis_index("seq"), lax.axis_index("head")
        self.z, self.col = self.s // 2, self.s % 2
        self.g, self.c = self.hd // 2, self.hd % 2
        self.sibling = (self.s, self.g * 2 + 1 - self.c)
        self.beside = (self.z * 2 + 1 - self.col, self.hd)
        self.above = (self.s + 2, self.hd)
        self.below = (self.s - 2, self.hd)


def remote(src, dst, send, recv, device):
    return pltpu.make_async_remote_copy(
        src_ref=src, dst_ref=dst, send_sem=send, recv_sem=recv, device_id=device, device_id_type=MESH)


def greet(w):
    barrier = pltpu.get_barrier_semaphore()

    def tell(device):
        pl.semaphore_signal(barrier, inc=1, device_id=device, device_id_type=MESH)

    def others(k, _):
        tell((w.s, (w.hd + k) % 16))
        return 0
    lax.fori_loop(1, 16, others, 0)
    tell(w.beside)

    @pl.when(w.z < 3)
    def _():
        tell(w.above)

    @pl.when(w.z > 0)
    def _():
        tell(w.below)


def await_greetings(w):
    pl.semaphore_wait(pltpu.get_barrier_semaphore(), 16 + (w.z + 2) // 3 + (5 - w.z) // 3)


def swap_copies(r, w):
    return (remote(r.query.at[1 - w.c], r.qraw.at[1], r.swap_send.at[0], r.swap_recv.at[0], w.sibling),
            remote(r.decay.at[1 - w.c], r.decay_raw.at[1], r.swap_send.at[1], r.swap_recv.at[1], w.sibling))


def spread(p):
    return (p % 256) // 32 * 64 + p // 256 * 32 + p % 32


CHUNKS = [(spread(32 * i), 32 * i) for i in range(16)]


def part(r, slot, j):
    return r.aux.at[slot] if j == 3 else r.kvb.at[slot, j]


def up_copy(r, w, step, j):
    return remote(part(r, 2 * step, j), part(r, 2 * step + 2, j), r.up_send.at[step, j], r.up_recv.at[step, j], w.above)


def side_copy(r, w, step, j):
    return remote(part(r, 2 * step + 2 * w.col, j), part(r, 2 * step + 1, j), r.side_send.at[step, j], r.side_recv.at[step, j], w.beside)


def sends_up(w, step):
    return (w.z < 3) if step == 0 else ((w.z >= 1) & (w.z < 3))


def sends_side(w, step):
    return w.z >= step + w.col


def gets_up(w, step):
    return w.z >= step + 1


def gets_side(w, step):
    return w.z >= step + 1 - w.col


def load_own(r, w):
    loads = [pltpu.make_async_copy(ref.at[w.c], r.raw.at[i], r.load_sem.at[i])
             for i, ref in enumerate((r.key, r.value, r.inner, r.outer))]
    qload = pltpu.make_async_copy(r.query.at[w.c], r.qraw.at[0], r.load_sem.at[4])
    aload = pltpu.make_async_copy(r.decay.at[w.c], r.decay_raw.at[0], r.load_sem.at[5])
    aload.start()
    for x in loads:
        x.start()
    qload.start()
    greet(w)
    swaps = swap_copies(r, w)

    def send_part(j):
        @pl.when(sends_up(w, 0))
        def _():
            up_copy(r, w, 0, j).start()

        @pl.when((w.col == 0) & sends_side(w, 0))
        def _():
            side_copy(r, w, 0, j).start()

    def send_small():
        aload.wait()
        swaps[1].wait_recv()
        mine, theirs = r.decay_raw[0], r.decay_raw[1]
        first = jnp.where(w.c == 0, mine, theirs)
        second = jnp.where(w.c == 0, theirs, mine)
        r.aux[0, 0:8, :] = jnp.concatenate([first, second], axis=0)
        docs = jnp.where(w.c == 0, r.docs[0:1, :], r.docs[1:2, :]).astype(F32)
        r.aux[0, 8:16, :] = jnp.broadcast_to(docs, (8, BLK))
        send_part(3)

    for i in range(4):
        loads[i].wait()
        r.wide[...] = r.raw[i].astype(F32)
        if i < 3:
            r.kvb[0, i] = r.wide[pl.ds(w.g, BLK, stride=8), :].astype(BF16)
            if i == 0:
                await_greetings(w)
                swaps[1].start()
            send_part(i)
            if i == 0:
                swaps[0].start()
            if i == 0:
                send_small()
        else:
            for pos, to in CHUNKS:
                r.outer_own[to:to + 32, :] = r.wide[pl.ds(w.g + 8 * pos, 32, stride=8), :].astype(BF16)
    qload.wait()
    swaps[0].wait_recv()
    for i in range(2):
        r.wide[0:2048, :] = r.qraw[i].astype(F32)
        base = 4 * w.c if i == 0 else 4 - 4 * w.c
        for j in range(4):
            for pos, to in CHUNKS:
                r.q[base + j, to:to + 32, :] = r.wide[pl.ds(j + 4 * pos, 32, stride=4), :].astype(BF16)
    for x in swaps:
        x.wait_send()


def take_up(r, w, step, parts):
    @pl.when(gets_up(w, step))
    def _():
        for j in parts:
            up_copy(r, w, step, j).wait_recv()
            if step == 0:
                @pl.when(w.col == 1)
                def _():
                    side_copy(r, w, 0, j).start()

                @pl.when(sends_up(w, 1))
                def _():
                    up_copy(r, w, 1, j).start()

                @pl.when(w.col == 0)
                def _():
                    side_copy(r, w, 1, j).start()
            else:
                @pl.when(w.col == 1)
                def _():
                    side_copy(r, w, 1, j).start()


def take_side(r, w, step, parts):
    for j in parts:
        side_copy(r, w, step, j).wait_recv()


def end_sends(r, w):
    for step in range(2):
        @pl.when(sends_up(w, step))
        def _():
            for j in range(4):
                up_copy(r, w, step, j).wait_send()

        @pl.when(sends_side(w, step))
        def _():
            for j in range(4):
                side_copy(r, w, step, j).wait_send()


def own_prepare(r):
    own = prefix_sums(r.aux[0, 0:8, :]) * LOG2E
    cols = to_columns(jnp.concatenate([own, r.aux[0, 8:16, :]], axis=0))
    r.csum_col[...] = cols
    rows = jnp.transpose(jnp.concatenate([cols[pos:pos + 32] for pos, _ in CHUNKS], axis=0))
    r.csum[...] = rows[0:8]
    r.docq[...] = rows[8:16]
    doc_c = cols[:, 8:9]
    cb = dot_nt(r.kvb[0, 2], r.outer_own[...])
    kj = lax.broadcasted_iota(jnp.int32, (BLK, BLK), 0)
    qi = spread(lax.broadcasted_iota(jnp.int32, (BLK, BLK), 1))
    seen = (qi >= kj) & (doc_c == r.docq[0:1, :])
    r.cb[...] = jnp.where(seen, cb, 0.0)
    r.hide[...] = jnp.where(seen, 0.0, -BIG)
    for slot in range(SLOTS):
        r.vt[slot, 128:144, :] = jnp.ones((16, BLK), BF16)
    r.vt[0, 0:128, :] = t16(r.kvb[0, 1])


def late(x):
    return jnp.concatenate([jnp.zeros_like(x), x], axis=1)


def own_half(r, qt, polls=()):
    base = qt * TQ
    parts = ((slice(0, 256), slice(0, 256)), (slice(256, 512), slice(128, 256)))
    cols = slice(base, base + TQ)
    polls = dict(polls)
    for at in range(2):
        r.pbuf[at, 256:512, 0:128] = jnp.zeros((256, 128), BF16)
        r.mbuf[at, 256:512, 0:128] = jnp.zeros((256, 128), BF16)

    def score(h):
        tops = []
        for keys, part_cols in parts:
            here = slice(base + part_cols.start, base + part_cols.stop)
            s = dot_nt(r.kvb[0, 0, keys, :], r.q[h, here, :]) + r.hide[keys, here]
            r.sbuf[h % 2, keys, part_cols] = s
            tops.append(jnp.max(s.reshape(32, 8, s.shape[1]), axis=0))
        both = jnp.concatenate([tops[0][:, 0:128], jnp.maximum(tops[0][:, 128:256], tops[1])], axis=1)
        return jnp.max(both, axis=0, keepdims=True)

    def soft(h, m):
        r.m[h, :, cols] = jnp.broadcast_to(m, (8, TQ))
        sums = []
        for keys, part_cols in parts:
            here = slice(base + part_cols.start, base + part_cols.stop)
            p = jnp.exp2((r.sbuf[h % 2, keys, part_cols] - m[:, part_cols]) * SC)
            fall = jnp.minimum(r.csum[h:h + 1, here] - r.csum_col[keys, h:h + 1], 0.0)
            mix = jnp.exp2(fall) * r.cb[keys, here]
            sums.append((fold_sum(p * p), fold_sum(p * mix), fold_sum(mix * mix)))
            r.pbuf[h % 2, keys, part_cols] = p.astype(BF16)
            r.mbuf[h % 2, keys, part_cols] = mix.astype(BF16)
        r.sq[h, :, cols], r.cross[h, :, cols], r.mixsq[h, :, cols] = (x + late(y) for x, y in zip(*sums))

    def apply(h):
        r.acc[h, 0:144, cols] = dot(r.vt[0], r.pbuf[h % 2])
        r.acc[h, 144:XR, cols] = jnp.zeros((128, TQ), F32)
        r.stud[h, :, cols] = dot(r.vt[0, 0:128, :], r.mbuf[h % 2])
        if qt == 0:
            r.state[h] = jnp.zeros((256, 128), F32)

    top = score(0)
    for h in range(HG):
        now = top
        if h + 1 < HG:
            top = score(h + 1)
        soft(h, now)
        if h > 0:
            apply(h - 1)
        if h in polls:
            polls[h]()
    apply(HG - 1)


def prepare(r, slot):
    sums = prefix_sums(r.aux[slot, 0:8, :])
    whole = sums[:, BLK - 1:BLK]
    doc_last = r.aux[1, 8:9, BLK - 1:BLK]
    tail = jnp.zeros((8, 1), F32)
    for t in range(1, slot):
        tail = tail + jnp.sum(r.aux[t, 0:8, :], axis=1, keepdims=True)
    weight = jnp.exp(whole - sums + tail)
    r.bdec[...] = jnp.where(r.aux[slot, 8:9, :] == doc_last, weight, 0.0)
    doc_c = to_columns(r.aux[slot, 8:16, :])[:, 0:1]
    r.kmask[slot] = jnp.broadcast_to(jnp.where(doc_c == doc_last, 0.0, -BIG), (BLK, 128))
    r.qoff[...] = jnp.broadcast_to(jnp.where(r.docq[0:1, :] == doc_last, 0.0, -BIG), (8, BLK))
    r.vt[slot, 0:128, :] = t16(r.kvb[slot, 1])
    r.bt[...] = t16(r.kvb[slot, 2]).astype(F32)


def slot_half(r, slot, qt, first, polls=()):
    base = qt * TQ
    cols = slice(base, base + TQ)
    far = slot == SLOTS - 1
    parts = ((slice(0, 256), slice(0, 128 if far else 256)), (slice(256, 512), slice(0, 256)))
    if far:
        for at in range(2):
            r.pbuf[at, 0:256, 128:256] = jnp.zeros((256, 128), BF16)

    def score(h):
        tops = []
        for keys, part_cols in parts:
            km = r.kmask[slot, keys, :]
            s = dot_nt(r.kvb[slot, 0, keys, :], r.q[h, base:base + part_cols.stop, :])
            s = s + jnp.concatenate([km] * (part_cols.stop // 128), axis=1)
            r.sbuf[h % 3, keys, part_cols] = s
            tops.append(jnp.max(s.reshape(32, 8, part_cols.stop), axis=0))
        if far:
            mx = jnp.concatenate([jnp.maximum(tops[0], tops[1][:, 0:128]), tops[1][:, 128:256]], axis=1)
        else:
            mx = jnp.maximum(*tops)
        return jnp.max(mx, axis=0, keepdims=True)

    def soft(h, top):
        qoff = r.qoff[0:1, cols]
        m_old = r.m[h, 0:1, cols]
        m = jnp.maximum(m_old, top + qoff)
        f = jnp.exp2((m_old - m) * SC)
        low = m - qoff
        r.m[h, :, cols] = jnp.broadcast_to(m, (8, TQ))
        r.cross[h, :, cols] = r.cross[h, :, cols] * f
        sq = r.sq[h, :, cols] * (f * f)
        for keys, part_cols in parts:
            p = jnp.exp2((r.sbuf[h % 3, keys, part_cols] - low[:, part_cols]) * SC)
            more = fold_sum(p * p)
            if part_cols.stop < TQ:
                more = jnp.concatenate([more, jnp.zeros_like(more)], axis=1)
            sq = sq + more
            r.pbuf[h % 2, keys, part_cols] = p.astype(BF16)
        r.sq[h, :, cols] = sq
        return f

    def extend(h):
        xb = (r.bt[...] * r.bdec[h:h + 1, :]).astype(BF16)
        r.xb[slot, h] = xb
        r.state[h] = r.state[h] + dot_nt(jnp.concatenate([r.vt[slot, 0:128, :], xb], axis=0), xb)

    def apply(h, f):
        both = jnp.concatenate([r.vt[slot], r.xb[slot, h]], axis=0)
        r.acc[h, :, cols] = r.acc[h, :, cols] * f + dot(both, r.pbuf[h % 2])

    polls = dict(polls)
    ahead = [score(h) for h in range(1 if first else 2)]
    kept = None
    for h in range(HG):
        if h + len(ahead) < HG:
            ahead.append(score(h + len(ahead)))
        f = soft(h, ahead.pop(0))
        if first:
            extend(h)
        if h > 0:
            apply(h - 1, kept)
        kept = f
        if h in polls:
            polls[h]()
    apply(HG - 1, kept)


def finish_rows(r, w, qt):
    cols = slice(qt * TQ, (qt + 1) * TQ)
    doc_last = r.aux[1, 8:9, BLK - 1:BLK]
    r.from_prev[...] = jnp.where((r.docq[0:1, cols] == doc_last) & (w.s > 0), jnp.ones((8, TQ), F32), 0.0)
    r.ct[...] = t16(r.outer_own[cols, :]).astype(F32)
    r.ssq[qt] = jnp.zeros((8, TQ), F32)

    def head(i, _):
        for u in range(2):
            h = i * 2 + u
            a = jnp.exp2(r.csum[pl.ds(h, 1), cols]) * r.from_prev[0:1, :]
            y = dot_nt(r.state[h].astype(BF16), r.outer_own[cols, :])
            inv = 1.0 / r.acc[h, 128:129, cols]
            tf = r.acc[h, 0:128, cols] * inv
            sf = r.stud[h, :, cols] + a * y[0:128, :]
            r.acc[h, 0:128, cols] = tf
            r.stud[h, :, cols] = sf
            r.mixsq[h, :, cols] = (r.mixsq[h, :, cols] + (a * a) * fold_sum(y[128:256, :] * r.ct[...])
                                   - (2.0 * inv) * (r.cross[h, :, cols] + a * fold_sum(r.ct[...] * r.acc[h, 144:XR, cols]))
                                   + (inv * inv) * r.sq[h, :, cols])
            r.ssq[qt, 0:1, :] = r.ssq[qt, 0:1, :] + jnp.sum(fold_sum(tf * tf), axis=0, keepdims=True)
            r.ssq[qt, 1:2, :] = r.ssq[qt, 1:2, :] + jnp.sum(fold_sum(sf * sf), axis=0, keepdims=True)
        return 0
    lax.fori_loop(0, HG // 2, head, 0)


def finish_layout(r, qt):
    cols = slice(qt * TQ, (qt + 1) * TQ)

    def head(h, _):
        r.teach[h, cols, :] = t16(r.acc[h, 0:128, cols].astype(BF16))
        r.student[h, cols, :] = t16(r.stud[h, :, cols].astype(BF16))
        r.err[pl.ds(h, 1), cols] = jnp.sum(r.mixsq[h, :, cols], axis=0, keepdims=True)
        return 0
    lax.fori_loop(0, HG, head, 0)


def ssq_copy(r, w, qt, k):
    return remote(r.ssq.at[qt], r.ssq_all.at[qt, w.g], r.ssq_send.at[qt, k], r.ssq_recv.at[qt, w.g],
                  (w.s, ((w.g + k) % 8) * 2 + w.c))


def ssq_from(r, w, qt, k):
    g = (w.g + 8 - k) % 8
    return remote(r.ssq.at[qt], r.ssq_all.at[qt, g], r.ssq_send.at[qt, k], r.ssq_recv.at[qt, g], (w.s, g * 2 + w.c))


def send_ssq(r, w, qt):
    for k in range(1, 8):
        ssq_copy(r, w, qt, k).start()
    r.ssq_all[qt, pl.ds(w.g, 1)] = r.ssq[qt].reshape(1, 8, TQ)


def gap_rows(qt, chip):
    return pl.ds(pl.multiple_of(qt * TQ + chip * 32, 32), 32)


def gap_lanes(g):
    return pl.ds(pl.multiple_of(g * 1024, 1024), 1024)


def gap_copy(r, w, qt, chip):
    to = chip * 2 + qt
    return remote(r.gap.at[gap_rows(qt, chip)], r.out.at[w.c, :, gap_lanes(w.g)],
                  r.out_send.at[to], r.out_recv.at[w.hd], (w.s, to))


def gap_stay(r, w):
    return pltpu.make_async_copy(r.gap.at[gap_rows(w.c, w.g)], r.out.at[w.c, :, gap_lanes(w.g)], r.out_send.at[w.hd])


def send_gap(r, w, qt):
    for k in range(1, 8):
        ssq_from(r, w, qt, k).wait_recv()
    sums = jnp.sum(r.ssq_all[qt], axis=0)
    r.scale[...] = to_columns(lax.rsqrt(sums / (8.0 * HG * 128) + EPS))
    gain = r.gain[pl.ds(pl.multiple_of(w.g * 1024, 1024), 1024)].reshape(1, 1024)

    def one(k, _):
        chip = (w.g + k) % 8
        rows = gap_rows(qt, chip)
        scale = r.scale[pl.ds(pl.multiple_of(chip * 32, 32), 32), :]
        t_scale, s_scale = scale[:, 0:1], scale[:, 1:2]
        for h in range(HG):
            lanes = slice(h * 128, (h + 1) * 128)
            gap = gain[:, lanes] * r.student[h, rows, :].astype(F32) * s_scale - r.teach[h, rows, :].astype(F32) * t_scale
            r.gap[rows, lanes] = gap.astype(BF16)
        stays = (k == 8) & (w.c == qt)

        @pl.when(stays)
        def _():
            gap_stay(r, w).start()

        @pl.when(jnp.logical_not(stays))
        def _():
            gap_copy(r, w, qt, chip).start()
        return 0
    lax.fori_loop(1, 9, one, 0)


def err_copy(r, w, seq):
    return remote(r.err_pair.at[1], r.err_out.at[seq], r.swap_send.at[2], r.swap_recv.at[2], w.sibling)


def send_err(r, w):
    cols = to_columns(r.err[...])
    back = sorted((pos, at) for pos, at in CHUNKS)
    err = jnp.transpose(jnp.concatenate([cols[at:at + 32] for _, at in back], axis=0))
    top, bottom = err[0:4, :], err[4:8, :]
    r.err_pair[0] = jnp.where(w.c == 0, top, bottom)
    r.err_pair[1] = jnp.where(w.c == 0, bottom, top)
    err_copy(r, w, w.c).start()
    near = pltpu.make_async_copy(r.err_pair.at[0], r.err_out.at[w.c], r.load_sem.at[0])
    near.start()
    near.wait()


def end_share(r, w):
    gap_stay(r, w).wait()
    err_copy(r, w, w.c).wait_send()
    err_copy(r, w, 1 - w.c).wait_recv()
    for k in range(1, 8):
        for qt in range(2):
            ssq_copy(r, w, qt, k).wait_send()

    def arrived(k, _):
        sender = (w.hd + k) % 16
        remote(r.gap.at[0:32], r.out.at[sender % 2, :, gap_lanes(sender // 2)],
               r.out_send.at[sender], r.out_recv.at[sender], (w.s, sender)).wait_recv()
        gap_copy(r, w, sender % 2, sender // 2).wait_send()
        return 0
    lax.fori_loop(1, 16, arrived, 0)


ARGS = ("query", "key", "value", "inner", "outer", "decay", "docs", "gain")
OUTS = ("out", "err_out")
DMA = pltpu.SemaphoreType.DMA
SCRATCH = dict(
    qraw=pltpu.VMEM((2, 2048, 128), BF16), decay_raw=pltpu.VMEM((2, 4, BLK), F32),
    raw=pltpu.VMEM((4, 4096, 128), BF16), wide=pltpu.VMEM((4096, 128), F32),
    q=pltpu.VMEM((HG, BLK, 128), BF16), kvb=pltpu.VMEM((SLOTS, 3, BLK, 128), BF16),
    aux=pltpu.VMEM((SLOTS, 16, BLK), F32), outer_own=pltpu.VMEM((BLK, 128), BF16),
    csum=pltpu.VMEM((8, BLK), F32), csum_col=pltpu.VMEM((BLK, 128), F32), docq=pltpu.VMEM((8, BLK), F32),
    cb=pltpu.VMEM((BLK, BLK), F32), hide=pltpu.VMEM((BLK, BLK), F32),
    m=pltpu.VMEM((HG, 8, BLK), F32), sq=pltpu.VMEM((HG, 8, BLK), F32),
    cross=pltpu.VMEM((HG, 8, BLK), F32), mixsq=pltpu.VMEM((HG, 8, BLK), F32),
    acc=pltpu.VMEM((HG, XR, BLK), F32), stud=pltpu.VMEM((HG, 128, BLK), F32),
    state=pltpu.VMEM((HG, 256, 128), F32), bdec=pltpu.VMEM((8, BLK), F32),
    kmask=pltpu.VMEM((SLOTS, BLK, 128), F32), qoff=pltpu.VMEM((8, BLK), F32),
    vt=pltpu.VMEM((SLOTS, 144, BLK), BF16), xb=pltpu.VMEM((SLOTS, HG, 128, BLK), BF16), bt=pltpu.VMEM((128, BLK), F32),
    sbuf=pltpu.VMEM((3, BLK, TQ), F32), pbuf=pltpu.VMEM((2, BLK, TQ), BF16), mbuf=pltpu.VMEM((2, BLK, TQ), BF16),
    ct=pltpu.VMEM((128, TQ), F32), from_prev=pltpu.VMEM((8, TQ), F32), scale=pltpu.VMEM((TQ, 128), F32),
    teach=pltpu.VMEM((HG, BLK, 128), BF16), student=pltpu.VMEM((HG, BLK, 128), BF16),
    err=pltpu.VMEM((8, BLK), F32), err_pair=pltpu.VMEM((2, 4, BLK), F32),
    ssq=pltpu.VMEM((2, 8, TQ), F32), ssq_all=pltpu.VMEM((2, 8, 8, TQ), F32), gap=pltpu.VMEM((BLK, HG * 128), BF16),
    load_sem=DMA((6,)), swap_send=DMA((3,)), swap_recv=DMA((3,)),
    up_send=DMA((2, 4)), up_recv=DMA((2, 4)), side_send=DMA((2, 4)), side_recv=DMA((2, 4)),
    ssq_send=DMA((2, 8)), ssq_recv=DMA((2, 8)), out_send=DMA((16,)), out_recv=DMA((16,)),
)


def kernel(*refs):
    r = Refs()
    for name, ref in zip(ARGS + OUTS + tuple(SCRATCH), refs):
        setattr(r, name, ref)
    w = Place()
    load_own(r, w)
    own_prepare(r)
    own_half(r, 0, {4: lambda: take_up(r, w, 0, (0, 3))})
    own_half(r, 1, {0: lambda: take_up(r, w, 0, (1,)), 7: lambda: take_up(r, w, 0, (2,))})

    @pl.when(w.s == 0)
    def _():
        r.aux[1] = jnp.zeros((16, BLK), F32)

    @pl.when(gets_side(w, 0))
    def _():
        side_copy(r, w, 0, 3).wait_recv()

    @pl.when(w.s >= 2)
    def _():
        prepare(r, 2)
        slot_half(r, 2, 0, True, {7: lambda: take_up(r, w, 1, (0, 3))})
        slot_half(r, 2, 1, False, {7: lambda: take_up(r, w, 1, (1,))})

    @pl.when(w.s >= 1)
    def _():
        take_side(r, w, 0, (0, 1, 2))
        prepare(r, 1)
        slot_half(r, 1, 0, True)
        slot_half(r, 1, 1, False, {0: lambda: take_up(r, w, 1, (2,))})

    @pl.when(w.s >= 3)
    def _():
        take_side(r, w, 1, (3,))

    @pl.when(w.s >= 4)
    def _():
        prepare(r, 4)
        slot_half(r, 4, 0, True)

    @pl.when(w.s >= 3)
    def _():
        take_side(r, w, 1, (0, 1, 2))
        prepare(r, 3)
        slot_half(r, 3, 0, True)
    finish_rows(r, w, 0)
    send_ssq(r, w, 0)
    finish_layout(r, 0)

    @pl.when(w.s >= 4)
    def _():
        slot_half(r, 4, 1, False, {4: lambda: send_gap(r, w, 0)})

    @pl.when(w.s < 4)
    def _():
        send_gap(r, w, 0)

    @pl.when(w.s >= 3)
    def _():
        slot_half(r, 3, 1, False)
    finish_rows(r, w, 1)
    send_ssq(r, w, 1)
    finish_layout(r, 1)
    send_err(r, w)
    send_gap(r, w, 1)
    end_share(r, w)
    end_sends(r, w)


def on_device(query_rows, key_rows, value_rows, state_in, state_out, log_decay, doc_ids, norm_gain):
    flat = [x.reshape(2, -1, 128) for x in (query_rows, key_rows, value_rows, state_in, state_out)]
    shapes = (jax.ShapeDtypeStruct((2, 32, 8192), BF16), jax.ShapeDtypeStruct((2, 4, BLK), F32))
    landed = pl.pallas_call(
        kernel,
        out_shape=(pltpu.VMEM(shapes[0].shape, BF16), shapes[1]),
        in_specs=[pl.BlockSpec(memory_space=pl.ANY)] * 6 + [pl.BlockSpec(memory_space=pltpu.VMEM)] * 2,
        out_specs=(pl.BlockSpec(memory_space=pltpu.VMEM), pl.BlockSpec(memory_space=pl.ANY)),
        scratch_shapes=list(SCRATCH.values()),
        compiler_params=pltpu.CompilerParams(collective_id=0, has_side_effects=True, vmem_limit_bytes=56 * 2**20),
        cost_estimate=pl.CostEstimate(flops=10**10, bytes_accessed=10**7, transcendentals=0),
    )(*flat, log_decay, doc_ids, norm_gain)
    return landed


def solution(mesh):
    placed = (
        P(None, "seq", "head", None),
        P(None, "seq", None, None),
        P(None, "seq", None, None),
        P(None, "seq", None, None),
        P(None, "seq", None, None),
        P(None, "head", "seq"),
        P(None, "seq"),
        P(),
    )
    return jax.shard_map(
        on_device,
        mesh=mesh,
        in_specs=placed,
        out_specs=(P(None, ("seq", "head"), None), P(None, "head", "seq")),
        check_vma=False,
    )
```

```python
import math

import jax
import jax.numpy as jnp
from jax import lax
from jax.experimental import pallas as pl
from jax.experimental.pallas import tpu as pltpu
from jax.sharding import PartitionSpec as P

F32, BF16 = jnp.float32, jnp.bfloat16
BLK, HG, SLOTS, TQ = 512, 8, 5, 256
XR = 272
LOG2E = 1.4426950408889634
SC = LOG2E / math.sqrt(128.0)
BIG = 1e30
EPS = 1e-05
NT = (((1,), (1,)), ((), ()))
MESH = pl.DeviceIdType.MESH


def dot_nt(a, b):
    return lax.dot_general(a, b, NT, preferred_element_type=F32)


def dot(a, b):
    return jnp.dot(a, b, preferred_element_type=F32)


def fold_sum(x):
    return jnp.sum(x.reshape(x.shape[0] // 8, 8, x.shape[1]), axis=0)


def fold_max(x):
    return jnp.max(jnp.max(x.reshape(x.shape[0] // 8, 8, x.shape[1]), axis=0), axis=0, keepdims=True)


def prefix_sums(x):
    lane = lax.broadcasted_iota(jnp.int32, x.shape, 1)
    step = 1
    while step < x.shape[1]:
        x = x + jnp.where(lane >= step, pltpu.roll(x, step, 1), 0.0)
        step *= 2
    return x


def to_columns(rows):
    wide = jnp.concatenate([rows, jnp.zeros((128 - rows.shape[0], rows.shape[1]), F32)], axis=0)
    return jnp.transpose(wide)


def t16(x):
    return jnp.transpose(x)


class Refs:
    pass


class Place:
    def __init__(self):
        self.s, self.hd = lax.axis_index("seq"), lax.axis_index("head")
        self.z, self.col = self.s // 2, self.s % 2
        self.g, self.c = self.hd // 2, self.hd % 2
        self.sibling = (self.s, self.g * 2 + 1 - self.c)
        self.beside = (self.z * 2 + 1 - self.col, self.hd)
        self.above = (self.s + 2, self.hd)
        self.below = (self.s - 2, self.hd)


def remote(src, dst, send, recv, device):
    return pltpu.make_async_remote_copy(
        src_ref=src, dst_ref=dst, send_sem=send, recv_sem=recv, device_id=device, device_id_type=MESH)


def greet(w):
    barrier = pltpu.get_barrier_semaphore()

    def tell(device):
        pl.semaphore_signal(barrier, inc=1, device_id=device, device_id_type=MESH)

    def others(k, _):
        tell((w.s, (w.hd + k) % 16))
        return 0
    lax.fori_loop(1, 16, others, 0)
    tell(w.beside)

    @pl.when(w.z < 3)
    def _():
        tell(w.above)

    @pl.when(w.z > 0)
    def _():
        tell(w.below)


def await_greetings(w):
    pl.semaphore_wait(pltpu.get_barrier_semaphore(), 16 + (w.z + 2) // 3 + (5 - w.z) // 3)


def swap_copies(r, w):
    return (remote(r.query.at[1 - w.c], r.qraw.at[1], r.swap_send.at[0], r.swap_recv.at[0], w.sibling),
            remote(r.decay.at[1 - w.c], r.decay_raw.at[1], r.swap_send.at[1], r.swap_recv.at[1], w.sibling))


def spread(p):
    return (p % 256) // 32 * 64 + p // 256 * 32 + p % 32


CHUNKS = [(spread(32 * i), 32 * i) for i in range(16)]


def part(r, slot, j):
    return r.aux.at[slot] if j == 3 else r.kvb.at[slot, j]


def up_copy(r, w, step, j):
    return remote(part(r, 2 * step, j), part(r, 2 * step + 2, j), r.up_send.at[step, j], r.up_recv.at[step, j], w.above)


def side_copy(r, w, step, j):
    return remote(part(r, 2 * step + 2 * w.col, j), part(r, 2 * step + 1, j), r.side_send.at[step, j], r.side_recv.at[step, j], w.beside)


def sends_up(w, step):
    return (w.z < 3) if step == 0 else ((w.z >= 1) & (w.z < 3))


def sends_side(w, step):
    return w.z >= step + w.col


def gets_up(w, step):
    return w.z >= step + 1


def gets_side(w, step):
    return w.z >= step + 1 - w.col


def load_own(r, w):
    loads = [pltpu.make_async_copy(ref.at[w.c], r.raw.at[i], r.load_sem.at[i])
             for i, ref in enumerate((r.key, r.value, r.inner, r.outer))]
    qload = pltpu.make_async_copy(r.query.at[w.c], r.qraw.at[0], r.load_sem.at[4])
    aload = pltpu.make_async_copy(r.decay.at[w.c], r.decay_raw.at[0], r.load_sem.at[5])
    aload.start()
    for x in loads:
        x.start()
    qload.start()
    greet(w)
    swaps = swap_copies(r, w)

    def send_part(j):
        @pl.when(sends_up(w, 0))
        def _():
            up_copy(r, w, 0, j).start()

        @pl.when((w.col == 0) & sends_side(w, 0))
        def _():
            side_copy(r, w, 0, j).start()

    def send_small():
        aload.wait()
        swaps[1].wait_recv()
        mine, theirs = r.decay_raw[0], r.decay_raw[1]
        first = jnp.where(w.c == 0, mine, theirs)
        second = jnp.where(w.c == 0, theirs, mine)
        r.aux[0, 0:8, :] = jnp.concatenate([first, second], axis=0)
        docs = jnp.where(w.c == 0, r.docs[0:1, :], r.docs[1:2, :]).astype(F32)
        r.aux[0, 8:16, :] = jnp.broadcast_to(docs, (8, BLK))
        send_part(3)

    for i in range(4):
        loads[i].wait()
        r.wide[0:4096, :] = r.raw[i].astype(F32)
        if i < 3:
            r.kvb[0, i] = r.wide[pl.ds(w.g, BLK, stride=8), :].astype(BF16)
            if i == 0:
                await_greetings(w)
                swaps[1].start()
            send_part(i)
            if i == 0:
                swaps[0].start()
            if i == 0:
                send_small()
        else:
            for pos, to in CHUNKS:
                r.outer_own[to:to + 32, :] = r.wide[pl.ds(w.g + 8 * pos, 32, stride=8), :].astype(BF16)
    qload.wait()
    swaps[0].wait_recv()
    for i in range(2):
        r.wide[0:2048, :] = r.qraw[i].astype(F32)
        base = 4 * w.c if i == 0 else 4 - 4 * w.c
        for j in range(4):
            for pos, to in CHUNKS:
                r.q[base + j, to:to + 32, :] = r.wide[pl.ds(j + 4 * pos, 32, stride=4), :].astype(BF16)
    for x in swaps:
        x.wait_send()


def take_up(r, w, step, parts):
    @pl.when(gets_up(w, step))
    def _():
        for j in parts:
            up_copy(r, w, step, j).wait_recv()
            if step == 0:
                @pl.when(w.col == 1)
                def _():
                    side_copy(r, w, 0, j).start()

                @pl.when(sends_up(w, 1))
                def _():
                    up_copy(r, w, 1, j).start()

                @pl.when(w.col == 0)
                def _():
                    side_copy(r, w, 1, j).start()
            else:
                @pl.when(w.col == 1)
                def _():
                    side_copy(r, w, 1, j).start()


def take_side(r, w, step, parts):
    for j in parts:
        side_copy(r, w, step, j).wait_recv()


def end_sends(r, w):
    for step in range(2):
        @pl.when(sends_up(w, step))
        def _():
            for j in range(4):
                up_copy(r, w, step, j).wait_send()

        @pl.when(sends_side(w, step))
        def _():
            for j in range(4):
                side_copy(r, w, step, j).wait_send()


def own_prepare(r):
    own = prefix_sums(r.aux[0, 0:8, :]) * LOG2E
    cols = to_columns(jnp.concatenate([own, r.aux[0, 8:16, :]], axis=0))
    r.csum_col[...] = cols
    rows = jnp.transpose(jnp.concatenate([cols[pos:pos + 32] for pos, _ in CHUNKS], axis=0))
    r.csum[...] = rows[0:8]
    r.docq[...] = rows[8:16]
    doc_c = cols[:, 8:9]
    cb = dot_nt(r.kvb[0, 2], r.outer_own[...])
    kj = lax.broadcasted_iota(jnp.int32, (BLK, BLK), 0)
    qi = spread(lax.broadcasted_iota(jnp.int32, (BLK, BLK), 1))
    seen = (qi >= kj) & (doc_c == r.docq[0:1, :])
    r.cb[...] = jnp.where(seen, cb, 0.0)
    r.hide[...] = jnp.where(seen, 0.0, -BIG)
    for slot in range(SLOTS):
        r.vt[slot, 128:144, :] = jnp.ones((16, BLK), BF16)
    r.vt[0, 0:128, :] = t16(r.kvb[0, 1])


def late(x):
    return jnp.concatenate([jnp.zeros_like(x), x], axis=1)


def own_half(r, qt, polls=()):
    base = qt * TQ
    parts = ((slice(0, 256), slice(0, 256)), (slice(256, 512), slice(128, 256)))
    cols = slice(base, base + TQ)
    polls = dict(polls)
    for at in range(2):
        r.pbuf[at, 256:512, 0:128] = jnp.zeros((256, 128), BF16)
        r.mbuf[at, 256:512, 0:128] = jnp.zeros((256, 128), BF16)

    def score(h):
        tops = []
        for keys, part_cols in parts:
            here = slice(base + part_cols.start, base + part_cols.stop)
            s = dot_nt(r.kvb[0, 0, keys, :], r.q[h, here, :]) + r.hide[keys, here]
            r.sbuf[h % 2, keys, part_cols] = s
            tops.append(jnp.max(s.reshape(32, 8, s.shape[1]), axis=0))
        both = jnp.concatenate([tops[0][:, 0:128], jnp.maximum(tops[0][:, 128:256], tops[1])], axis=1)
        return jnp.max(both, axis=0, keepdims=True)

    def soft(h, m):
        r.m[h, :, cols] = jnp.broadcast_to(m, (8, TQ))
        sums = []
        for keys, part_cols in parts:
            here = slice(base + part_cols.start, base + part_cols.stop)
            p = jnp.exp2((r.sbuf[h % 2, keys, part_cols] - m[:, part_cols]) * SC)
            fall = jnp.minimum(r.csum[h:h + 1, here] - r.csum_col[keys, h:h + 1], 0.0)
            mix = jnp.exp2(fall) * r.cb[keys, here]
            sums.append((fold_sum(p * p), fold_sum(p * mix), fold_sum(mix * mix)))
            r.pbuf[h % 2, keys, part_cols] = p.astype(BF16)
            r.mbuf[h % 2, keys, part_cols] = mix.astype(BF16)
        r.sq[h, :, cols], r.cross[h, :, cols], r.mixsq[h, :, cols] = (x + late(y) for x, y in zip(*sums))

    def apply(h):
        r.acc[h, 0:144, cols] = dot(r.vt[0], r.pbuf[h % 2])
        r.acc[h, 144:XR, cols] = jnp.zeros((128, TQ), F32)
        r.stud[h, :, cols] = dot(r.vt[0, 0:128, :], r.mbuf[h % 2])
        if qt == 0:
            r.state[h] = jnp.zeros((256, 128), F32)

    top = score(0)
    for h in range(HG):
        now = top
        if h + 1 < HG:
            top = score(h + 1)
        soft(h, now)
        if h > 0:
            apply(h - 1)
        if h in polls:
            polls[h]()
    apply(HG - 1)


def prepare(r, slot):
    sums = prefix_sums(r.aux[slot, 0:8, :])
    whole = sums[:, BLK - 1:BLK]
    doc_last = r.aux[1, 8:9, BLK - 1:BLK]
    tail = jnp.zeros((8, 1), F32)
    for t in range(1, slot):
        tail = tail + jnp.sum(r.aux[t, 0:8, :], axis=1, keepdims=True)
    weight = jnp.exp(whole - sums + tail)
    r.bdec[...] = jnp.where(r.aux[slot, 8:9, :] == doc_last, weight, 0.0)
    doc_c = to_columns(r.aux[slot, 8:16, :])[:, 0:1]
    r.kmask[slot] = jnp.broadcast_to(jnp.where(doc_c == doc_last, 0.0, -BIG), (BLK, 128))
    r.qoff[...] = jnp.broadcast_to(jnp.where(r.docq[0:1, :] == doc_last, 0.0, -BIG), (8, BLK))
    r.vt[slot, 0:128, :] = t16(r.kvb[slot, 1])
    r.bt[...] = t16(r.kvb[slot, 2]).astype(F32)


def slot_half(r, slot, qt, first, polls=()):
    base = qt * TQ
    cols = slice(base, base + TQ)
    far = slot == SLOTS - 1
    parts = ((slice(0, 256), slice(0, 128 if far else 256)), (slice(256, 512), slice(0, 256)))
    if far:
        for at in range(2):
            r.pbuf[at, 0:256, 128:256] = jnp.zeros((256, 128), BF16)

    def score(h):
        tops = []
        for keys, part_cols in parts:
            km = r.kmask[slot, keys, :]
            s = dot_nt(r.kvb[slot, 0, keys, :], r.q[h, base:base + part_cols.stop, :])
            s = s + jnp.concatenate([km] * (part_cols.stop // 128), axis=1)
            r.sbuf[h % 3, keys, part_cols] = s
            tops.append(jnp.max(s.reshape(32, 8, part_cols.stop), axis=0))
        if far:
            mx = jnp.concatenate([jnp.maximum(tops[0], tops[1][:, 0:128]), tops[1][:, 128:256]], axis=1)
        else:
            mx = jnp.maximum(*tops)
        return jnp.max(mx, axis=0, keepdims=True)

    def soft(h, top):
        qoff = r.qoff[0:1, cols]
        m_old = r.m[h, 0:1, cols]
        m = jnp.maximum(m_old, top + qoff)
        f = jnp.exp2((m_old - m) * SC)
        low = m - qoff
        r.m[h, :, cols] = jnp.broadcast_to(m, (8, TQ))
        r.cross[h, :, cols] = r.cross[h, :, cols] * f
        sq = r.sq[h, :, cols] * (f * f)
        for keys, part_cols in parts:
            p = jnp.exp2((r.sbuf[h % 3, keys, part_cols] - low[:, part_cols]) * SC)
            more = fold_sum(p * p)
            if part_cols.stop < TQ:
                more = jnp.concatenate([more, jnp.zeros_like(more)], axis=1)
            sq = sq + more
            r.pbuf[h % 2, keys, part_cols] = p.astype(BF16)
        r.sq[h, :, cols] = sq
        return f

    def extend(h):
        xb = (r.bt[...] * r.bdec[h:h + 1, :]).astype(BF16)
        r.xb[slot, h] = xb
        r.state[h] = r.state[h] + dot_nt(jnp.concatenate([r.vt[slot, 0:128, :], xb], axis=0), xb)

    def apply(h, f):
        both = jnp.concatenate([r.vt[slot], r.xb[slot, h]], axis=0)
        r.acc[h, :, cols] = r.acc[h, :, cols] * f + dot(both, r.pbuf[h % 2])

    polls = dict(polls)
    ahead = [score(h) for h in range(1 if first else 2)]
    kept = None
    for h in range(HG):
        if h + len(ahead) < HG:
            ahead.append(score(h + len(ahead)))
        f = soft(h, ahead.pop(0))
        if first:
            extend(h)
        if h > 0:
            apply(h - 1, kept)
        kept = f
        if h in polls:
            polls[h]()
    apply(HG - 1, kept)


def finish_rows(r, w, qt):
    cols = slice(qt * TQ, (qt + 1) * TQ)
    doc_last = r.aux[1, 8:9, BLK - 1:BLK]
    r.from_prev[...] = jnp.where((r.docq[0:1, cols] == doc_last) & (w.s > 0), jnp.ones((8, TQ), F32), 0.0)
    r.ct[...] = t16(r.outer_own[cols, :]).astype(F32)
    r.ssq[qt] = jnp.zeros((8, TQ), F32)

    def head(i, _):
        for u in range(2):
            h = i * 2 + u
            a = jnp.exp2(r.csum[pl.ds(h, 1), cols]) * r.from_prev[0:1, :]
            y = dot_nt(r.state[h].astype(BF16), r.outer_own[cols, :])
            inv = 1.0 / r.acc[h, 128:129, cols]
            tf = r.acc[h, 0:128, cols] * inv
            sf = r.stud[h, :, cols] + a * y[0:128, :]
            r.acc[h, 0:128, cols] = tf
            r.stud[h, :, cols] = sf
            r.mixsq[h, :, cols] = (r.mixsq[h, :, cols] + (a * a) * fold_sum(y[128:256, :] * r.ct[...])
                                   - (2.0 * inv) * (r.cross[h, :, cols] + a * fold_sum(r.ct[...] * r.acc[h, 144:XR, cols]))
                                   + (inv * inv) * r.sq[h, :, cols])
            r.ssq[qt, 0:1, :] = r.ssq[qt, 0:1, :] + jnp.sum(fold_sum(tf * tf), axis=0, keepdims=True)
            r.ssq[qt, 1:2, :] = r.ssq[qt, 1:2, :] + jnp.sum(fold_sum(sf * sf), axis=0, keepdims=True)
        return 0
    lax.fori_loop(0, HG // 2, head, 0)


def finish_layout(r, qt):
    cols = slice(qt * TQ, (qt + 1) * TQ)

    def head(h, _):
        r.teach[h, cols, :] = t16(r.acc[h, 0:128, cols].astype(BF16))
        r.student[h, cols, :] = t16(r.stud[h, :, cols].astype(BF16))
        r.err[pl.ds(h, 1), cols] = jnp.sum(r.mixsq[h, :, cols], axis=0, keepdims=True)
        return 0
    lax.fori_loop(0, HG, head, 0)


def ssq_copy(r, w, qt, k):
    return remote(r.ssq.at[qt], r.ssq_all.at[qt, w.g], r.ssq_send.at[qt, k], r.ssq_recv.at[qt, w.g],
                  (w.s, ((w.g + k) % 8) * 2 + w.c))


def ssq_from(r, w, qt, k):
    g = (w.g + 8 - k) % 8
    return remote(r.ssq.at[qt], r.ssq_all.at[qt, g], r.ssq_send.at[qt, k], r.ssq_recv.at[qt, g], (w.s, g * 2 + w.c))


def send_ssq(r, w, qt):
    for k in range(1, 8):
        ssq_copy(r, w, qt, k).start()
    r.ssq_all[qt, pl.ds(w.g, 1)] = r.ssq[qt].reshape(1, 8, TQ)


def gap_rows(qt, chip):
    return pl.ds(pl.multiple_of(qt * TQ + chip * 32, 32), 32)


def gap_lanes(g):
    return pl.ds(pl.multiple_of(g * 1024, 1024), 1024)


def gap_copy(r, w, qt, chip):
    to = chip * 2 + qt
    return remote(r.gap.at[gap_rows(qt, chip)], r.out.at[w.c, :, gap_lanes(w.g)],
                  r.out_send.at[to], r.out_recv.at[w.hd], (w.s, to))


def gap_stay(r, w):
    return pltpu.make_async_copy(r.gap.at[gap_rows(w.c, w.g)], r.out.at[w.c, :, gap_lanes(w.g)], r.out_send.at[w.hd])


def send_gap(r, w, qt):
    for k in range(1, 8):
        ssq_from(r, w, qt, k).wait_recv()
    sums = jnp.sum(r.ssq_all[qt], axis=0)
    r.scale[...] = to_columns(lax.rsqrt(sums / (8.0 * HG * 128) + EPS))
    gain = r.gain[pl.ds(pl.multiple_of(w.g * 1024, 1024), 1024)].reshape(1, 1024)

    def one(k, _):
        chip = (w.g + k) % 8
        rows = gap_rows(qt, chip)
        scale = r.scale[pl.ds(pl.multiple_of(chip * 32, 32), 32), :]
        t_scale, s_scale = scale[:, 0:1], scale[:, 1:2]
        for h in range(HG):
            lanes = slice(h * 128, (h + 1) * 128)
            gap = gain[:, lanes] * r.student[h, rows, :].astype(F32) * s_scale - r.teach[h, rows, :].astype(F32) * t_scale
            r.gap[rows, lanes] = gap.astype(BF16)
        stays = (k == 8) & (w.c == qt)

        @pl.when(stays)
        def _():
            gap_stay(r, w).start()

        @pl.when(jnp.logical_not(stays))
        def _():
            gap_copy(r, w, qt, chip).start()
        return 0
    lax.fori_loop(1, 9, one, 0)


def err_copy(r, w, seq):
    return remote(r.err_pair.at[1], r.err_out.at[seq], r.swap_send.at[2], r.swap_recv.at[2], w.sibling)


def send_err(r, w):
    cols = to_columns(r.err[...])
    back = sorted((pos, at) for pos, at in CHUNKS)
    err = jnp.transpose(jnp.concatenate([cols[at:at + 32] for _, at in back], axis=0))
    top, bottom = err[0:4, :], err[4:8, :]
    r.err_pair[0] = jnp.where(w.c == 0, top, bottom)
    r.err_pair[1] = jnp.where(w.c == 0, bottom, top)
    err_copy(r, w, w.c).start()
    near = pltpu.make_async_copy(r.err_pair.at[0], r.err_out.at[w.c], r.load_sem.at[0])
    near.start()
    near.wait()


def end_share(r, w):
    gap_stay(r, w).wait()
    err_copy(r, w, w.c).wait_send()
    err_copy(r, w, 1 - w.c).wait_recv()
    for k in range(1, 8):
        for qt in range(2):
            ssq_copy(r, w, qt, k).wait_send()

    def arrived(k, _):
        sender = (w.hd + k) % 16
        remote(r.gap.at[0:32], r.out.at[sender % 2, :, gap_lanes(sender // 2)],
               r.out_send.at[sender], r.out_recv.at[sender], (w.s, sender)).wait_recv()
        gap_copy(r, w, sender % 2, sender // 2).wait_send()
        return 0
    lax.fori_loop(1, 16, arrived, 0)


ARGS = ("query", "key", "value", "inner", "outer", "decay", "docs", "gain")
OUTS = ("out", "err_out")
DMA = pltpu.SemaphoreType.DMA
SCRATCH = dict(
    qraw=pltpu.VMEM((2, 2048, 128), BF16), decay_raw=pltpu.VMEM((2, 4, BLK), F32),
    raw=pltpu.VMEM((4, 4096, 128), BF16), wide=pltpu.VMEM((4104, 128), F32),
    q=pltpu.VMEM((HG, BLK, 128), BF16), kvb=pltpu.VMEM((SLOTS, 3, BLK, 128), BF16),
    aux=pltpu.VMEM((SLOTS, 16, BLK), F32), outer_own=pltpu.VMEM((BLK, 128), BF16),
    csum=pltpu.VMEM((8, BLK), F32), csum_col=pltpu.VMEM((BLK, 128), F32), docq=pltpu.VMEM((8, BLK), F32),
    cb=pltpu.VMEM((BLK, BLK), F32), hide=pltpu.VMEM((BLK, BLK), F32),
    m=pltpu.VMEM((HG, 8, BLK), F32), sq=pltpu.VMEM((HG, 8, BLK), F32),
    cross=pltpu.VMEM((HG, 8, BLK), F32), mixsq=pltpu.VMEM((HG, 8, BLK), F32),
    acc=pltpu.VMEM((HG, XR, BLK), F32), stud=pltpu.VMEM((HG, 128, BLK), F32),
    state=pltpu.VMEM((HG, 256, 128), F32), bdec=pltpu.VMEM((8, BLK), F32),
    kmask=pltpu.VMEM((SLOTS, BLK, 128), F32), qoff=pltpu.VMEM((8, BLK), F32),
    vt=pltpu.VMEM((SLOTS, 144, BLK), BF16), xb=pltpu.VMEM((SLOTS, HG, 128, BLK), BF16), bt=pltpu.VMEM((128, BLK), F32),
    sbuf=pltpu.VMEM((3, BLK, TQ), F32), pbuf=pltpu.VMEM((2, BLK, TQ), BF16), mbuf=pltpu.VMEM((2, BLK, TQ), BF16),
    ct=pltpu.VMEM((128, TQ), F32), from_prev=pltpu.VMEM((8, TQ), F32), scale=pltpu.VMEM((TQ, 128), F32),
    teach=pltpu.VMEM((HG, BLK, 128), BF16), student=pltpu.VMEM((HG, BLK, 128), BF16),
    err=pltpu.VMEM((8, BLK), F32), err_pair=pltpu.VMEM((2, 4, BLK), F32),
    ssq=pltpu.VMEM((2, 8, TQ), F32), ssq_all=pltpu.VMEM((2, 8, 8, TQ), F32), gap=pltpu.VMEM((BLK, HG * 128), BF16),
    load_sem=DMA((6,)), swap_send=DMA((3,)), swap_recv=DMA((3,)),
    up_send=DMA((2, 4)), up_recv=DMA((2, 4)), side_send=DMA((2, 4)), side_recv=DMA((2, 4)),
    ssq_send=DMA((2, 8)), ssq_recv=DMA((2, 8)), out_send=DMA((16,)), out_recv=DMA((16,)),
)


def kernel(*refs):
    r = Refs()
    for name, ref in zip(ARGS + OUTS + tuple(SCRATCH), refs):
        setattr(r, name, ref)
    w = Place()
    load_own(r, w)
    own_prepare(r)
    own_half(r, 0, {4: lambda: take_up(r, w, 0, (0, 3))})
    own_half(r, 1, {0: lambda: take_up(r, w, 0, (1,)), 7: lambda: take_up(r, w, 0, (2,))})

    @pl.when(w.s == 0)
    def _():
        r.aux[1] = jnp.zeros((16, BLK), F32)

    @pl.when(gets_side(w, 0))
    def _():
        side_copy(r, w, 0, 3).wait_recv()

    @pl.when(w.s >= 2)
    def _():
        prepare(r, 2)
        slot_half(r, 2, 0, True, {7: lambda: take_up(r, w, 1, (0, 3))})
        slot_half(r, 2, 1, False, {7: lambda: take_up(r, w, 1, (1,))})

    @pl.when(w.s >= 1)
    def _():
        take_side(r, w, 0, (0, 1, 2))
        prepare(r, 1)
        slot_half(r, 1, 0, True)
        slot_half(r, 1, 1, False, {0: lambda: take_up(r, w, 1, (2,))})

    @pl.when(w.s >= 3)
    def _():
        take_side(r, w, 1, (3,))

    @pl.when(w.s >= 4)
    def _():
        prepare(r, 4)
        slot_half(r, 4, 0, True)

    @pl.when(w.s >= 3)
    def _():
        take_side(r, w, 1, (0, 1, 2))
        prepare(r, 3)
        slot_half(r, 3, 0, True)
    finish_rows(r, w, 0)
    send_ssq(r, w, 0)
    finish_layout(r, 0)

    @pl.when(w.s >= 4)
    def _():
        slot_half(r, 4, 1, False, {4: lambda: send_gap(r, w, 0)})

    @pl.when(w.s < 4)
    def _():
        send_gap(r, w, 0)

    @pl.when(w.s >= 3)
    def _():
        slot_half(r, 3, 1, False)
    finish_rows(r, w, 1)
    send_ssq(r, w, 1)
    finish_layout(r, 1)
    send_err(r, w)
    send_gap(r, w, 1)
    end_share(r, w)
    end_sends(r, w)


def on_device(query_rows, key_rows, value_rows, state_in, state_out, log_decay, doc_ids, norm_gain):
    flat = [x.reshape(2, -1, 128) for x in (query_rows, key_rows, value_rows, state_in, state_out)]
    shapes = (jax.ShapeDtypeStruct((2, 32, 8192), BF16), jax.ShapeDtypeStruct((2, 4, BLK), F32))
    landed = pl.pallas_call(
        kernel,
        out_shape=(pltpu.VMEM(shapes[0].shape, BF16), shapes[1]),
        in_specs=[pl.BlockSpec(memory_space=pl.ANY)] * 6 + [pl.BlockSpec(memory_space=pltpu.VMEM)] * 2,
        out_specs=(pl.BlockSpec(memory_space=pltpu.VMEM), pl.BlockSpec(memory_space=pl.ANY)),
        scratch_shapes=list(SCRATCH.values()),
        compiler_params=pltpu.CompilerParams(collective_id=0, has_side_effects=True, vmem_limit_bytes=56 * 2**20),
        cost_estimate=pl.CostEstimate(flops=10**10, bytes_accessed=10**7, transcendentals=0),
    )(*flat, log_decay, doc_ids, norm_gain)
    return landed


def solution(mesh):
    placed = (
        P(None, "seq", "head", None),
        P(None, "seq", None, None),
        P(None, "seq", None, None),
        P(None, "seq", None, None),
        P(None, "seq", None, None),
        P(None, "head", "seq"),
        P(None, "seq"),
        P(),
    )
    return jax.shard_map(
        on_device,
        mesh=mesh,
        in_specs=placed,
        out_specs=(P(None, ("seq", "head"), None), P(None, "head", "seq")),
        check_vma=False,
    )
```
